128 devices in a mesh: gx: 8 (over x_hi, z), gy: 16 (over x_lo, y, core).
Axes of the slice: x: 4 (x_hi: 2, x_lo: 2; x = x_hi * 2 + x_lo), y: 4, z: 4, core: 2. Of those that a mesh axis runs over, the one named last changes fastest.
Arguments:
- object_field: float32 [2, 2, 1024, 2048], P(None, None, 'gx', 'gy'), may hold values from -1 to 1
- probe: float32 [2, 128, 128], replicated, may hold values from -0.5 to 0.5
- propagator: float32 [128, 128], replicated, may hold values from -3.140625 to 3.140625
- offsets: int32 [8, 16, 12, 2], P('gx', 'gy'), may hold values from 0 to 128
- counts: int32 [8, 16], P('gx', 'gy'), may hold values from 1 to 12, as said below
- intensity: float32 [8, 16, 12, 128, 128], P('gx', 'gy'), may hold values from 0.1 to 4
Outputs:
- updated_object: float32 [2, 2, 1024, 2048], P(None, None, 'gx', 'gy')
The draws below stay inside these ranges and needn't reach their ends.
Inputs may be any that keep to these rules, and one draw needn't show every extreme that they name: `counts`: some tile has all 12 slots live in every draw; positions are live in slot order.
All inputs are finite; a program needn't handle non-finite values.
Results may differ from the reference program's by a relative error of at most 0.0003.
Values sent between devices are 32-bit elements; how exact they have to be, the bound alone decides.
A program may use at most 64 MiB of HBM per device.

```python
import math
import jax
import jax.numpy as jnp
from jax import lax

PROBE = 128
HALO = 64
TILE = 128
BATCH = 2
NB = 6
POS = 12
TILES_X = 8
TILES_Y = 16
NX = 1024
NY = 2048


def draw_counts(key, part):
    keys = jax.random.split(jax.random.fold_in(key, 7), 2)
    values = jax.random.randint(keys[0], (TILES_X * TILES_Y,), 1, POS + 1, dtype=jnp.int32)
    chosen = jax.random.randint(keys[1], (), 0, TILES_X * TILES_Y, dtype=jnp.int32)
    values = values.at[chosen].set(POS)
    return values.reshape(TILES_X, TILES_Y)


def with_ends(array, rng, least, largest):
    extent = array.shape
    spot = [jax.random.randint(jax.random.fold_in(rng, axis), (), 0, extent[axis]) for axis in range(len(extent))]
    array = array.at[tuple(spot)].set(least)
    longest = extent.index(max(extent))
    spot[longest] = (spot[longest] + 1) % extent[longest]
    return array.at[tuple(spot)].set(largest)


def block_levels(own_key, extent, pieces, smallest, largest):
    loudness = 1.0
    for position, parts in pieces:
        steps = jax.random.uniform(jax.random.fold_in(jax.random.fold_in(own_key, 6), position), (parts,), jnp.float32, smallest / len(pieces), largest / len(pieces))
        loudness = loudness * jnp.repeat(jnp.exp(steps), extent[position] // parts).reshape((-1,) + (1,) * (len(extent) - 1 - position))
    return loudness


def setup_inputs(seed: int = 0) -> dict:
    splits = jax.random.split(jax.random.key(seed), 7)
    return {
        "object_field": jnp.clip(jax.random.uniform(splits[0], (2, 2, NX, NY), jnp.float32, -1.0, 1.0) * block_levels(splits[0], (2, 2, NX, NY), ((2, 8), (3, 16)), -0.4, 0.0), -1.0, 1.0),
        "probe": jnp.clip(jax.random.uniform(splits[1], (2, PROBE, PROBE), jnp.float32, -0.5, 0.5), -0.5, 0.5),
        "propagator": jnp.clip(jax.random.uniform(splits[2], (PROBE, PROBE), jnp.float32, -3.140625, 3.140625), -3.140625, 3.140625),
        "offsets": with_ends(jax.random.randint(splits[3], (TILES_X, TILES_Y, POS, 2), 0, TILE + 1), jax.random.fold_in(splits[3], 1), 0, TILE).astype(jnp.int32),
        "counts": draw_counts(jax.random.fold_in(splits[6], 71), 0),
        "intensity": jnp.clip(jnp.exp(math.log(4.0) - 3.6888794 * jax.random.uniform(splits[5], (TILES_X, TILES_Y, POS, PROBE, PROBE), jnp.float32) ** block_levels(splits[5], (TILES_X, TILES_Y, POS, PROBE, PROBE), ((0, 8), (1, 16)), -0.2, 0.2)), 0.1, 4.0),
    }


def product(first, second):
    return (first[0] * second[0] - first[1] * second[1], first[0] * second[1] + first[1] * second[0])

def conjugate(field):
    return (field[0], -field[1])

def tables(width):
    index = jnp.arange(width, dtype=jnp.int32)
    phase = (index[:, None] * index[None, :] % width).astype(jnp.float32) * (2.0 * math.pi / width)
    return (jnp.cos(phase) / math.sqrt(width), jnp.sin(phase) / math.sqrt(width))

def left_mul(matrix, field):
    return jnp.einsum('ij,...jk->...ik', matrix, field, precision=lax.Precision.HIGHEST)

def right_mul(field, matrix):
    return jnp.einsum('...ij,jk->...ik', field, matrix, precision=lax.Precision.HIGHEST)

def transform(field, basis, direction):
    cosine = basis[0]
    signed = direction * basis[1]
    first_real = left_mul(cosine, field[0]) - left_mul(signed, field[1])
    first_imag = left_mul(cosine, field[1]) + left_mul(signed, field[0])
    return (right_mul(first_real, cosine) - right_mul(first_imag, signed), right_mul(first_imag, cosine) + right_mul(first_real, signed))

def gradients(probe_pair, wave_pair, patches, measured, basis):
    slice_one = (patches[:, 0, 0], patches[:, 0, 1])
    slice_two = (patches[:, 1, 0], patches[:, 1, 1])
    entrance = product(probe_pair, slice_one)
    spectrum = product(transform(entrance, basis, -1.0), wave_pair)
    inner_wave = transform(spectrum, basis, 1.0)
    farfield = transform(product(inner_wave, slice_two), basis, -1.0)
    excess = farfield[0] * farfield[0] + farfield[1] * farfield[1] - measured
    back_exit = transform((excess * farfield[0], excess * farfield[1]), basis, 1.0)
    grad_two = product(conjugate(inner_wave), back_exit)
    back_inner = product(conjugate(slice_two), back_exit)
    back_spec = product(conjugate(wave_pair), transform(back_inner, basis, -1.0))
    grad_one = product(conjugate(probe_pair), transform(back_spec, basis, 1.0))
    return jnp.stack([jnp.stack(grad_one, 1), jnp.stack(grad_two, 1)], 1)

def reference(object_field, probe, propagator, offsets, counts, intensity):
    width = PROBE
    margin = HALO
    basis = tables(width)
    probe_pair = (probe[0], probe[1])
    wave_pair = (jnp.cos(propagator), jnp.sin(propagator))
    field = object_field
    zero = jnp.zeros((), jnp.int32)
    for period in range(NB):
        padded = jnp.pad(field, ((0, 0), (0, 0), (margin, margin), (margin, margin)))
        first_slot = period * BATCH

        def visit(total, tile_number):
            row_tile = (tile_number // TILES_Y).astype(jnp.int32)
            col_tile = (tile_number % TILES_Y).astype(jnp.int32)
            starts = []
            patches = []
            for member in range(BATCH):
                row_start = (row_tile * TILE + offsets[row_tile, col_tile, first_slot + member, 0]).astype(jnp.int32)
                col_start = (col_tile * TILE + offsets[row_tile, col_tile, first_slot + member, 1]).astype(jnp.int32)
                starts.append((zero, zero, row_start, col_start))
                patches.append(lax.dynamic_slice(padded, (zero, zero, row_start, col_start), (2, 2, width, width)))
            measured = intensity[row_tile, col_tile, first_slot:first_slot + BATCH]
            live = first_slot + jnp.arange(BATCH, dtype=jnp.int32) < counts[row_tile, col_tile]
            grads = gradients(probe_pair, wave_pair, jnp.stack(patches), measured, basis)
            grads = grads * live.astype(jnp.float32)[:, None, None, None, None]
            for member in range(BATCH):
                current = lax.dynamic_slice(total, starts[member], (2, 2, width, width))
                total = lax.dynamic_update_slice(total, current + grads[member], starts[member])
            return (total, None)
        total, _ = lax.scan(visit, jnp.zeros_like(padded), jnp.arange(TILES_X * TILES_Y, dtype=jnp.int32))
        field = field - 0.08 * total[:, :, margin:-margin, margin:-margin]
    return field
```

```python
import math

import jax
import jax.numpy as jnp
import ml_dtypes
import numpy as np
from jax import lax
from jax.experimental import pallas as pl
from jax.experimental.pallas import tpu as pltpu
from jax.sharding import PartitionSpec as P

MESH = pl.DeviceIdType.MESH
N = 128
H = 64
BATCH = 2
NB = 6
STEP = 0.08
F32 = jnp.float32
BF16 = jnp.bfloat16

Y_RE, Z_IM, M_RS, Z_M, Z_RE, Y_IM = range(6)
K_YRE, K_ZIM_U, K_ZIM_D, K_M, K_ZM_U, K_ZM_D, K_ZRE_U, K_ZRE_D, K_YIM, K_P3 = range(10)
TOP = pl.ds(0, N)
BOT = pl.ds(N, N)


def dft_tables():
    index = np.arange(N)
    phase = (index[:, None] * index[None, :] % N) * (2.0 * math.pi / N)
    c, s = np.cos(phase) / math.sqrt(N), np.sin(phase) / math.sqrt(N)
    rights, lefts = [], []
    for sign in (-1.0, 1.0):
        right = np.block([[c, sign * s], [-sign * s, c]])
        left = right.T
        for m, out, axis in ((right, rights, 0), (left, lefts, 1)):
            hi = m.astype(ml_dtypes.bfloat16)
            lo = (m - hi.astype(np.float64)).astype(ml_dtypes.bfloat16)
            out.append(np.concatenate([hi, hi, lo], axis=axis))
    return np.stack(rights), np.stack(lefts)


def cmul(ar, ai, br, bi):
    return ar * br - ai * bi, ar * bi + ai * br


def kernel(offs, cnt, obj, probe, prop, inten, wr, wl, out, o0, o1, d, z, r, a, q, psi, pat, ssem, rsem):
    objects = (o0, o1)
    gx = lax.axis_index("gx")
    gy = lax.axis_index("gy")
    core = lax.rem(gy, 2)
    has_u = gx > 0
    has_d = gx < 7
    has_o = jnp.logical_and(gy > 0, gy < 15)
    up = (jnp.maximum(gx - 1, 0), gy)
    dn = (jnp.minimum(gx + 1, 7), gy)
    mate = (gx, gy + 1 - 2 * core)
    outer = (gx, jnp.clip(gy - 1 + 2 * core, 0, 15))
    hl = 1 - core
    hr = core

    lane = lax.broadcasted_iota(jnp.int32, (1, N), 1)
    row = lax.broadcasted_iota(jnp.int32, (2 * N, N), 0)
    row_ok = jnp.logical_and(row >= jnp.where(gx == 0, H, 0), row < jnp.where(gx == 7, 3 * H, 4 * H))
    l_ok = lane >= jnp.where(gy == 0, H, 0)
    r_ok = lane < jnp.where(gy == 15, H, N)

    def desc(kind, src, dst, s, slot, dev):
        return pltpu.make_async_remote_copy(
            src_ref=src,
            dst_ref=dst,
            send_sem=ssem.at[kind, s, slot],
            recv_sem=rsem.at[kind, s, slot],
            device_id=dev,
            device_id_type=MESH,
        )

    def copy(kind, s, slot):
        if kind == K_YRE:
            return desc(kind, d.at[s, 1, 0], r.at[Y_RE, s, slot], s, slot, outer)
        if kind == K_ZIM_U:
            return desc(kind, d.at[s, 1, 1, TOP], r.at[Z_IM, s, slot, BOT], s, slot, up)
        if kind == K_ZIM_D:
            return desc(kind, d.at[s, 1, 1, BOT], r.at[Z_IM, s, slot, TOP], s, slot, dn)
        if kind == K_M:
            return desc(kind, d.at[s, 0, 1 - core], r.at[M_RS, s, slot], s, slot, mate)
        if kind == K_ZM_U:
            return desc(kind, a.at[2, s, TOP], r.at[Z_M, s, slot, BOT], s, slot, up)
        if kind == K_ZM_D:
            return desc(kind, a.at[2, s, BOT], r.at[Z_M, s, slot, TOP], s, slot, dn)
        if kind == K_ZRE_U:
            return desc(kind, a.at[0, s, TOP], r.at[Z_RE, s, slot, BOT], s, slot, up)
        if kind == K_ZRE_D:
            return desc(kind, a.at[0, s, BOT], r.at[Z_RE, s, slot, TOP], s, slot, dn)
        if kind == K_YIM:
            return desc(kind, a.at[1, s], r.at[Y_IM, s, slot], s, slot, outer)
        return desc(kind, objects[s].at[0, core], objects[s].at[0, core], s, slot, mate)

    senders = {
        K_YRE: has_o, K_ZIM_U: has_u, K_ZIM_D: has_d, K_M: None, K_ZM_U: has_u, K_ZM_D: has_d,
        K_ZRE_U: has_u, K_ZRE_D: has_d, K_YIM: has_o, K_P3: None,
    }
    receivers = dict(senders)
    for ku, kd in ((K_ZIM_U, K_ZIM_D), (K_ZM_U, K_ZM_D), (K_ZRE_U, K_ZRE_D)):
        receivers[ku], receivers[kd] = has_d, has_u

    def guarded(cond, fn):
        if cond is None:
            fn()
        else:
            pl.when(cond)(fn)

    def send(kind, s, slot):
        guarded(senders[kind], lambda: copy(kind, s, slot).start())

    def recv(kind, s, slot):
        if kind == K_P3:
            desc(kind, objects[s].at[0, core], objects[s].at[0, 1 - core], s, slot, mate).wait_recv()
        else:
            guarded(receivers[kind], lambda: copy(kind, s, slot).wait_recv())

    def sent(kind, s, slot):
        guarded(senders[kind], lambda: copy(kind, s, slot).wait_send())

    def start(s, slot):
        send(K_M, s, slot)
        send(K_YRE, s, slot)
        send(K_ZIM_U, s, slot)
        send(K_ZIM_D, s, slot)

    def mid_m(s, slot):
        recv(K_M, s, slot)
        a[2, s] = d[s, 0, core] + r[M_RS, s, slot]
        send(K_ZM_U, s, slot)
        send(K_ZM_D, s, slot)

    def mid_re(s, slot):
        recv(K_YRE, s, slot)
        a[0, s] = d[s, 1, 0] + r[Y_RE, s, slot]
        send(K_ZRE_U, s, slot)
        send(K_ZRE_D, s, slot)

    def mid_im(s, slot):
        recv(K_ZIM_U, s, slot)
        recv(K_ZIM_D, s, slot)
        a[1, s] = d[s, 1, 1] + r[Z_IM, s, slot]
        send(K_YIM, s, slot)

    def mid_back(s, slot):
        recv(K_ZM_U, s, slot)
        recv(K_ZM_D, s, slot)
        objects[s][0, core] = objects[s][0, core] + (a[2, s] + r[Z_M, s, slot])
        send(K_P3, s, slot)

    def finish(s, slot):
        recv(K_ZRE_U, s, slot)
        recv(K_ZRE_D, s, slot)
        objects[s][1, 0] = objects[s][1, 0] + (a[0, s] + r[Z_RE, s, slot])
        recv(K_YIM, s, slot)
        objects[s][1, 1] = objects[s][1, 1] + (a[1, s] + r[Y_IM, s, slot])
        recv(K_P3, s, slot)
        for kind in range(10):
            sent(kind, s, slot)

    def exchange(slot):
        mid_m(1, slot)
        mid_m(0, slot)
        mid_re(1, slot)
        mid_im(1, slot)
        mid_re(0, slot)
        mid_im(0, slot)
        mid_back(0, slot)
        mid_back(1, slot)
        finish(0, slot)

    r[...] = jnp.zeros_like(r)
    for o in objects:
        o[...] = jnp.zeros_like(o)
    d[...] = jnp.zeros_like(d)
    z[...] = jnp.zeros_like(z)
    barrier = pltpu.get_barrier_semaphore()
    for cond, dev in ((None, mate), (has_u, up), (has_d, dn), (has_o, outer)):
        guarded(cond, lambda dev=dev: pl.semaphore_signal(barrier, inc=1, device_id=dev, device_id_type=MESH))
    count = 1 + has_u.astype(jnp.int32) + has_d.astype(jnp.int32) + has_o.astype(jnp.int32)
    pl.semaphore_wait(barrier, count)

    for s in (1, 0):
        for c in range(2):
            tile = pltpu.roll(obj[s, c], H, 1)
            d[s, hl, c, pl.ds(H, N)] = jnp.where(lane >= H, tile, 0.0)
            d[s, hr, c, pl.ds(H, N)] = jnp.where(lane < H, tile, 0.0)
        start(s, 0)
    q[0] = jnp.cos(prop[...])
    q[1] = jnp.sin(prop[...])
    exchange(0)

    def split(x):
        hi = x.astype(BF16)
        return hi, (x - hi.astype(F32)).astype(BF16)

    def transform(re, im, inverse):
        x = jnp.concatenate([jnp.concatenate([re[m], im[m]], 1) for m in range(BATCH)], 0)
        hi, lo = split(x)
        y = jnp.dot(jnp.concatenate([hi, lo, hi], 1), wr[inverse], preferred_element_type=F32)
        x = jnp.concatenate(
            [jnp.concatenate([y[:N, :N], y[N:, :N]], 1), jnp.concatenate([y[:N, N:], y[N:, N:]], 1)], 0
        )
        hi, lo = split(x)
        y = jnp.dot(wl[inverse], jnp.concatenate([hi, lo, hi], 0), preferred_element_type=F32)
        return (y[:N, :N], y[:N, N:]), (y[N:, :N], y[N:, N:])

    def patch(s, c, r0, q0):
        left = objects[s][hl, c, pl.ds(r0, N), :]
        right = objects[s][hr, c, pl.ds(r0, N), :]
        return pltpu.roll(jnp.where(lane >= q0, left, right), (N - q0) & (N - 1), 1)

    def scatter(s, places, grads):
        for m in range(BATCH):
            r0, q0, weight = places[m]
            fl = jnp.where(jnp.logical_and(lane >= q0, l_ok), weight, 0.0)
            fr = jnp.where(jnp.logical_and(lane < q0, r_ok), weight, 0.0)
            for c in range(2):
                g = pltpu.roll(grads[c][m], q0 & (N - 1), 1)
                z[m, 0, c, pl.ds(N, N)] = g * fl
                z[m, 1, c, pl.ds(N, N)] = g * fr
        for h, half in ((0, hl), (1, hr)):
            for c in range(2):
                total = z[0, h, c, pl.ds(N - places[0][0], 2 * N), :] + z[1, h, c, pl.ds(N - places[1][0], 2 * N), :]
                d[s, half, c] = jnp.where(row_ok, total, 0.0)

    def batch(b, carry):
        slot = lax.rem(b + 1, 2)
        before = lax.rem(b, 2)
        places = []
        for m in range(BATCH):
            n = b * BATCH + m
            weight = jnp.where(n < cnt[0, 0], -STEP, 0.0).astype(F32)
            places.append((offs[n, 0], offs[n, 1], weight))
        pr, pi = probe[0], probe[1]
        re, im = [], []
        for m in range(BATCH):
            r0, q0, _ = places[m]
            x, y = cmul(pr, pi, patch(0, 0, r0, q0), patch(0, 1, r0, q0))
            re.append(x)
            im.append(y)
        re, im = transform(re, im, 0)
        both = [cmul(re[m], im[m], q[0], q[1]) for m in range(BATCH)]
        re, im = transform([x for x, _ in both], [y for _, y in both], 1)
        for m in range(BATCH):
            psi[m, 0] = re[m]
            psi[m, 1] = im[m]
        finish(1, before)
        both = []
        for m in range(BATCH):
            r0, q0, _ = places[m]
            for c in range(2):
                pat[m, c] = patch(1, c, r0, q0)
            both.append(cmul(psi[m, 0], psi[m, 1], pat[m, 0], pat[m, 1]))
        re, im = transform([x for x, _ in both], [y for _, y in both], 0)
        excess = [re[m] * re[m] + im[m] * im[m] - inten[b * BATCH + m] for m in range(BATCH)]
        re, im = transform([excess[m] * re[m] for m in range(BATCH)], [excess[m] * im[m] for m in range(BATCH)], 1)
        both = [cmul(psi[m, 0], -psi[m, 1], re[m], im[m]) for m in range(BATCH)]
        scatter(1, places, ([x for x, _ in both], [y for _, y in both]))
        start(1, slot)
        both = [cmul(pat[m, 0], -pat[m, 1], re[m], im[m]) for m in range(BATCH)]
        re, im = transform([x for x, _ in both], [y for _, y in both], 0)
        both = [cmul(re[m], im[m], q[0], -q[1]) for m in range(BATCH)]
        re, im = transform([x for x, _ in both], [y for _, y in both], 1)
        both = [cmul(re[m], im[m], pr, -pi) for m in range(BATCH)]
        scatter(0, places, ([x for x, _ in both], [y for _, y in both]))
        start(0, slot)
        exchange(slot)
        return carry

    lax.fori_loop(0, NB, batch, 0)
    finish(1, NB % 2)
    for s in range(2):
        for c in range(2):
            left = objects[s][hl, c, pl.ds(H, N), :]
            right = objects[s][hr, c, pl.ds(H, N), :]
            out[s, c] = pltpu.roll(jnp.where(lane >= H, left, right), H, 1)


def solution(mesh):
    rights, lefts = dft_tables()

    def local(object_field, probe, propagator, offsets, counts, intensity):
        vmem = pl.BlockSpec(memory_space=pltpu.VMEM)
        smem = pl.BlockSpec(memory_space=pltpu.SMEM)
        return pl.pallas_call(
            kernel,
            out_shape=jax.ShapeDtypeStruct((2, 2, N, N), F32),
            in_specs=[smem, smem] + [vmem] * 6,
            out_specs=vmem,
            scratch_shapes=[
                pltpu.VMEM((2, 2, 2 * N, N), F32),
                pltpu.VMEM((2, 2, 2 * N, N), F32),
                pltpu.VMEM((2, 2, 2, 2 * N, N), F32),
                pltpu.VMEM((BATCH, 2, 2, 3 * N, N), F32),
                pltpu.VMEM((6, 2, 2, 2 * N, N), F32),
                pltpu.VMEM((3, 2, 2 * N, N), F32),
                pltpu.VMEM((2, N, N), F32),
                pltpu.VMEM((BATCH, 2, N, N), F32),
                pltpu.VMEM((BATCH, 2, N, N), F32),
                pltpu.SemaphoreType.DMA((10, 2, 2)),
                pltpu.SemaphoreType.DMA((10, 2, 2)),
            ],
            compiler_params=pltpu.CompilerParams(
                collective_id=0, has_side_effects=True, vmem_limit_bytes=48 * 1024 * 1024
            ),
        )(
            offsets[0, 0], counts, object_field, probe, propagator, intensity[0, 0],
            jnp.asarray(rights), jnp.asarray(lefts),
        )

    in_specs = (
        P(None, None, "gx", "gy"),
        P(),
        P(),
        P("gx", "gy", None, None),
        P("gx", "gy"),
        P("gx", "gy", None, None, None),
    )
    out_specs = P(None, None, "gx", "gy")
    return jax.shard_map(local, mesh=mesh, in_specs=in_specs, out_specs=out_specs, check_vma=False)
```

```python
import math

import jax
import jax.numpy as jnp
import ml_dtypes
import numpy as np
from jax import lax
from jax.experimental import pallas as pl
from jax.experimental.pallas import tpu as pltpu
from jax.sharding import PartitionSpec as P

MESH = pl.DeviceIdType.MESH
N = 128
H = 64
BATCH = 2
NB = 6
STEP = 0.08
F32 = jnp.float32
BF16 = jnp.bfloat16

Y_RE, Z_IM, M_RS, Z_M, Z_RE, Y_IM = range(6)
K_YRE, K_ZIM_U, K_ZIM_D, K_M, K_ZM_U, K_ZM_D, K_ZRE_U, K_ZRE_D, K_YIM, K_P3 = range(10)
TOP = pl.ds(0, N)
BOT = pl.ds(N, N)


def dft_tables():
    index = np.arange(N)
    phase = (index[:, None] * index[None, :] % N) * (2.0 * math.pi / N)
    c, s = np.cos(phase) / math.sqrt(N), np.sin(phase) / math.sqrt(N)
    out = []
    for sign in (-1.0, 1.0):
        m = np.block([[c, sign * s], [-sign * s, c]])
        hi = m.astype(ml_dtypes.bfloat16)
        out.append(np.stack([hi, (m - hi.astype(np.float64)).astype(ml_dtypes.bfloat16)]))
    return np.stack(out)


def place(hi_x, lo_x, y, z, core):
    return hi_x * 4 + z, (lo_x * 4 + y) * 2 + core


def parts(gx, gy):
    return lax.div(gx, 4), lax.rem(gx, 4), lax.div(gy, 8), lax.rem(lax.div(gy, 2), 4), lax.rem(gy, 2)


def tile_of(gx, gy):
    hi_x, z, lo_x, y, core = parts(gx, gy)
    lo_x = lax.rem(lo_x + hi_x, 2)
    z = jnp.where(hi_x == 1, 3 - z, z)
    y = jnp.where(lo_x == 1, 3 - y, y)
    return place(hi_x, lo_x, y, z, core)


def device_of(gx, gy):
    hi_x, z, lo_x, y, core = parts(gx, gy)
    z = jnp.where(hi_x == 1, 3 - z, z)
    y = jnp.where(lo_x == 1, 3 - y, y)
    return place(hi_x, lax.rem(lo_x + hi_x, 2), y, z, core)


def cmul(ar, ai, br, bi):
    return ar * br - ai * bi, ar * bi + ai * br


def kernel(
    offs_in, cnt_in, obj, probe_in, prop_in, inten_in, w_in, out,
    o0, o1, d, z, r, a, q, psi, pat, tile, inten, fin, probe, prop, w, offs, cnt,
    ssem, rsem, in_send, in_recv, out_send, out_recv, lsem,
):
    objects = (o0, o1)
    me = (lax.axis_index("gx"), lax.axis_index("gy"))
    gx, gy = tile_of(*me)
    core = lax.rem(gy, 2)
    home = (gx, gy)
    worker = device_of(*me)
    moved = jnp.logical_or(gx != me[0], gy != me[1])
    stays = jnp.logical_not(moved)
    has_u = gx > 0
    has_d = gx < 7
    has_o = jnp.logical_and(gy > 0, gy < 15)
    up = device_of(jnp.maximum(gx - 1, 0), gy)
    dn = device_of(jnp.minimum(gx + 1, 7), gy)
    mate = device_of(gx, gy + 1 - 2 * core)
    outer = device_of(gx, jnp.clip(gy - 1 + 2 * core, 0, 15))
    hl = 1 - core
    hr = core

    lane = lax.broadcasted_iota(jnp.int32, (1, N), 1)
    row = lax.broadcasted_iota(jnp.int32, (2 * N, N), 0)
    row_ok = jnp.logical_and(row >= jnp.where(gx == 0, H, 0), row < jnp.where(gx == 7, 3 * H, 4 * H))
    l_ok = lane >= jnp.where(gy == 0, H, 0)
    r_ok = lane < jnp.where(gy == 15, H, N)

    def desc(kind, src, dst, s, slot, dev):
        return pltpu.make_async_remote_copy(
            src_ref=src,
            dst_ref=dst,
            send_sem=ssem.at[kind, s, slot],
            recv_sem=rsem.at[kind, s, slot],
            device_id=dev,
            device_id_type=MESH,
        )

    def copy(kind, s, slot):
        if kind == K_YRE:
            return desc(kind, d.at[s, 1, 0], r.at[Y_RE, s, slot], s, slot, outer)
        if kind == K_ZIM_U:
            return desc(kind, d.at[s, 1, 1, TOP], r.at[Z_IM, s, slot, BOT], s, slot, up)
        if kind == K_ZIM_D:
            return desc(kind, d.at[s, 1, 1, BOT], r.at[Z_IM, s, slot, TOP], s, slot, dn)
        if kind == K_M:
            return desc(kind, d.at[s, 0, 1 - core], r.at[M_RS, s, slot], s, slot, mate)
        if kind == K_ZM_U:
            return desc(kind, a.at[2, s, TOP], r.at[Z_M, s, slot, BOT], s, slot, up)
        if kind == K_ZM_D:
            return desc(kind, a.at[2, s, BOT], r.at[Z_M, s, slot, TOP], s, slot, dn)
        if kind == K_ZRE_U:
            return desc(kind, a.at[0, s, TOP], r.at[Z_RE, s, slot, BOT], s, slot, up)
        if kind == K_ZRE_D:
            return desc(kind, a.at[0, s, BOT], r.at[Z_RE, s, slot, TOP], s, slot, dn)
        if kind == K_YIM:
            return desc(kind, a.at[1, s], r.at[Y_IM, s, slot], s, slot, outer)
        return desc(kind, objects[s].at[0, core], objects[s].at[0, core], s, slot, mate)

    senders = {
        K_YRE: has_o, K_ZIM_U: has_u, K_ZIM_D: has_d, K_M: None, K_ZM_U: has_u, K_ZM_D: has_d,
        K_ZRE_U: has_u, K_ZRE_D: has_d, K_YIM: has_o, K_P3: None,
    }
    receivers = dict(senders)
    for ku, kd in ((K_ZIM_U, K_ZIM_D), (K_ZM_U, K_ZM_D), (K_ZRE_U, K_ZRE_D)):
        receivers[ku], receivers[kd] = has_d, has_u

    def guarded(cond, fn):
        if cond is None:
            fn()
        else:
            pl.when(cond)(fn)

    def send(kind, s, slot):
        guarded(senders[kind], lambda: copy(kind, s, slot).start())

    def recv(kind, s, slot):
        if kind == K_P3:
            desc(kind, objects[s].at[0, core], objects[s].at[0, 1 - core], s, slot, mate).wait_recv()
        else:
            guarded(receivers[kind], lambda: copy(kind, s, slot).wait_recv())

    def sent(kind, s, slot):
        guarded(senders[kind], lambda: copy(kind, s, slot).wait_send())

    def start(s, slot):
        send(K_M, s, slot)
        send(K_YRE, s, slot)
        send(K_ZIM_U, s, slot)
        send(K_ZIM_D, s, slot)

    def mid_m(s, slot):
        recv(K_M, s, slot)
        a[2, s] = d[s, 0, core] + r[M_RS, s, slot]
        send(K_ZM_U, s, slot)
        send(K_ZM_D, s, slot)

    def mid_re(s, slot):
        recv(K_YRE, s, slot)
        a[0, s] = d[s, 1, 0] + r[Y_RE, s, slot]
        send(K_ZRE_U, s, slot)
        send(K_ZRE_D, s, slot)

    def mid_im(s, slot):
        recv(K_ZIM_U, s, slot)
        recv(K_ZIM_D, s, slot)
        a[1, s] = d[s, 1, 1] + r[Z_IM, s, slot]
        send(K_YIM, s, slot)

    def mid_back(s, slot):
        recv(K_ZM_U, s, slot)
        recv(K_ZM_D, s, slot)
        objects[s][0, core] = objects[s][0, core] + (a[2, s] + r[Z_M, s, slot])
        send(K_P3, s, slot)

    def finish(s, slot):
        recv(K_ZRE_U, s, slot)
        recv(K_ZRE_D, s, slot)
        objects[s][1, 0] = objects[s][1, 0] + (a[0, s] + r[Z_RE, s, slot])
        recv(K_YIM, s, slot)
        objects[s][1, 1] = objects[s][1, 1] + (a[1, s] + r[Y_IM, s, slot])
        recv(K_P3, s, slot)
        for kind in range(10):
            sent(kind, s, slot)

    def exchange(slot):
        mid_m(1, slot)
        mid_m(0, slot)
        mid_re(1, slot)
        mid_im(1, slot)
        mid_re(0, slot)
        mid_im(0, slot)
        mid_back(0, slot)
        mid_back(1, slot)
        finish(0, slot)

    inputs = [(offs_in, offs), (cnt_in, cnt)]
    inputs += [(obj.at[s], tile.at[s]) for s in range(2)]

    def pass_on(i, src, dst):
        return pltpu.make_async_remote_copy(
            src_ref=src,
            dst_ref=dst,
            send_sem=in_send.at[i],
            recv_sem=in_recv.at[i],
            device_id=worker,
            device_id_type=MESH,
        )

    def keep(i, src, dst):
        return pltpu.make_async_copy(src, dst, in_send.at[i])

    def pass_start(i, src, dst):
        pl.when(moved)(lambda: pass_on(i, src, dst).start())
        pl.when(stays)(lambda: keep(i, src, dst).start())

    def pass_wait(i, src, dst):
        @pl.when(moved)
        def _():
            pass_on(i, src, dst).wait_send()
            pass_on(i, src, dst).wait_recv()

        pl.when(stays)(lambda: keep(i, src, dst).wait())

    def frames(b):
        return 4 + b, inten_in.at[pl.ds(BATCH * b, BATCH)], inten.at[pl.ds(BATCH * b, BATCH)]

    consts = [(probe_in, probe), (prop_in, prop), (w_in, w)]
    for i, (src, dst) in enumerate(consts):
        pltpu.make_async_copy(src, dst, lsem.at[i]).start()

    barrier = pltpu.get_barrier_semaphore()
    greet = ((None, mate), (has_u, up), (has_d, dn), (has_o, outer), (moved, home), (moved, worker))
    r[...] = jnp.zeros_like(r)
    for o in objects:
        o[...] = jnp.zeros_like(o)
    d[...] = jnp.zeros_like(d)
    z[...] = jnp.zeros_like(z)
    for cond, dev in greet:
        guarded(cond, lambda dev=dev: pl.semaphore_signal(barrier, inc=1, device_id=dev, device_id_type=MESH))
    count = 1 + sum(jnp.where(cond, 1, 0) for cond, _ in greet[1:])
    pl.semaphore_wait(barrier, count)
    for i in range(4):
        pass_start(i, *inputs[i])
    pass_start(*frames(0))

    for s in (0, 1):
        pass_wait(2 + s, *inputs[2 + s])
        for c in range(2):
            cells = pltpu.roll(tile[s, c], H, 1)
            d[s, hl, c, pl.ds(H, N)] = jnp.where(lane >= H, cells, 0.0)
            d[s, hr, c, pl.ds(H, N)] = jnp.where(lane < H, cells, 0.0)
        start(s, 0)
    for i, (src, dst) in enumerate(consts):
        pltpu.make_async_copy(src, dst, lsem.at[i]).wait()
    for i in range(2):
        pass_wait(i, *inputs[i])
    q[0] = jnp.cos(prop[...])
    q[1] = jnp.sin(prop[...])
    exchange(0)

    def split(x):
        hi = x.astype(BF16)
        return hi, (x - hi.astype(F32)).astype(BF16)

    def transform(re, im, inverse):
        x = jnp.concatenate([jnp.concatenate([re[m], im[m]], 1) for m in range(BATCH)], 0)
        hi, lo = split(x)
        right = jnp.concatenate([w[inverse, 0], w[inverse, 0], w[inverse, 1]], 0)
        y = jnp.dot(jnp.concatenate([hi, lo, hi], 1), right, preferred_element_type=F32)
        x = jnp.concatenate(
            [jnp.concatenate([y[:N, :N], y[N:, :N]], 1), jnp.concatenate([y[:N, N:], y[N:, N:]], 1)], 0
        )
        hi, lo = split(x)
        left = jnp.concatenate([w[1 - inverse, 0], w[1 - inverse, 0], w[1 - inverse, 1]], 1)
        y = jnp.dot(left, jnp.concatenate([hi, lo, hi], 0), preferred_element_type=F32)
        return (y[:N, :N], y[:N, N:]), (y[N:, :N], y[N:, N:])

    def patch(s, c, r0, q0):
        left = objects[s][hl, c, pl.ds(r0, N), :]
        right = objects[s][hr, c, pl.ds(r0, N), :]
        return pltpu.roll(jnp.where(lane >= q0, left, right), (N - q0) & (N - 1), 1)

    def scatter(s, places, grads):
        for m in range(BATCH):
            r0, q0, weight = places[m]
            fl = jnp.where(jnp.logical_and(lane >= q0, l_ok), weight, 0.0)
            fr = jnp.where(jnp.logical_and(lane < q0, r_ok), weight, 0.0)
            for c in range(2):
                g = pltpu.roll(grads[c][m], q0 & (N - 1), 1)
                z[m, 0, c, pl.ds(N, N)] = g * fl
                z[m, 1, c, pl.ds(N, N)] = g * fr
        for h, half in ((0, hl), (1, hr)):
            for c in range(2):
                total = z[0, h, c, pl.ds(N - places[0][0], 2 * N), :] + z[1, h, c, pl.ds(N - places[1][0], 2 * N), :]
                d[s, half, c] = jnp.where(row_ok, total, 0.0)

    def batch(b, carry):
        slot = lax.rem(b + 1, 2)
        before = lax.rem(b, 2)
        pl.when(b < NB - 1)(lambda: pass_start(*frames(b + 1)))
        places = []
        for m in range(BATCH):
            n = b * BATCH + m
            weight = jnp.where(n < cnt[0, 0], -STEP, 0.0).astype(F32)
            places.append((offs[0, n], offs[1, n], weight))
        pr, pi = probe[0], probe[1]
        re, im = [], []
        for m in range(BATCH):
            r0, q0, _ = places[m]
            x, y = cmul(pr, pi, patch(0, 0, r0, q0), patch(0, 1, r0, q0))
            re.append(x)
            im.append(y)
        re, im = transform(re, im, 0)
        both = [cmul(re[m], im[m], q[0], q[1]) for m in range(BATCH)]
        re, im = transform([x for x, _ in both], [y for _, y in both], 1)
        for m in range(BATCH):
            psi[m, 0] = re[m]
            psi[m, 1] = im[m]
        finish(1, before)
        both = []
        for m in range(BATCH):
            r0, q0, _ = places[m]
            for c in range(2):
                pat[m, c] = patch(1, c, r0, q0)
            both.append(cmul(psi[m, 0], psi[m, 1], pat[m, 0], pat[m, 1]))
        re, im = transform([x for x, _ in both], [y for _, y in both], 0)
        pass_wait(*frames(b))
        excess = [re[m] * re[m] + im[m] * im[m] - inten[b * BATCH + m] for m in range(BATCH)]
        re, im = transform([excess[m] * re[m] for m in range(BATCH)], [excess[m] * im[m] for m in range(BATCH)], 1)
        both = [cmul(psi[m, 0], -psi[m, 1], re[m], im[m]) for m in range(BATCH)]
        scatter(1, places, ([x for x, _ in both], [y for _, y in both]))
        start(1, slot)
        both = [cmul(pat[m, 0], -pat[m, 1], re[m], im[m]) for m in range(BATCH)]
        re, im = transform([x for x, _ in both], [y for _, y in both], 0)
        both = [cmul(re[m], im[m], q[0], -q[1]) for m in range(BATCH)]
        re, im = transform([x for x, _ in both], [y for _, y in both], 1)
        both = [cmul(re[m], im[m], pr, -pi) for m in range(BATCH)]
        scatter(0, places, ([x for x, _ in both], [y for _, y in both]))
        start(0, slot)
        exchange(slot)
        return carry

    def send_home(s):
        return pltpu.make_async_remote_copy(
            src_ref=fin.at[s],
            dst_ref=out.at[s],
            send_sem=out_send.at[s],
            recv_sem=out_recv.at[s],
            device_id=home,
            device_id_type=MESH,
        )

    def give(s):
        for c in range(2):
            left = objects[s][hl, c, pl.ds(H, N), :]
            right = objects[s][hr, c, pl.ds(H, N), :]
            fin[s, c] = pltpu.roll(jnp.where(lane >= H, left, right), H, 1)
        pl.when(moved)(lambda: send_home(s).start())

        @pl.when(stays)
        def _():
            out[s] = fin[s]

    lax.fori_loop(0, NB, batch, 0)
    give(0)
    finish(1, NB % 2)
    give(1)
    for s in range(2):
        @pl.when(moved)
        def _():
            send_home(s).wait_send()
            send_home(s).wait_recv()


def solution(mesh):
    tables = dft_tables()

    def local(object_field, probe, propagator, offsets, counts, intensity):
        hbm = pl.BlockSpec(memory_space=pltpu.HBM)
        return pl.pallas_call(
            kernel,
            out_shape=jax.ShapeDtypeStruct((2, 2, N, N), F32),
            in_specs=[hbm] * 7,
            out_specs=pl.BlockSpec(memory_space=pltpu.VMEM),
            scratch_shapes=[
                pltpu.VMEM((2, 2, 2 * N, N), F32),
                pltpu.VMEM((2, 2, 2 * N, N), F32),
                pltpu.VMEM((2, 2, 2, 2 * N, N), F32),
                pltpu.VMEM((BATCH, 2, 2, 3 * N, N), F32),
                pltpu.VMEM((6, 2, 2, 2 * N, N), F32),
                pltpu.VMEM((3, 2, 2 * N, N), F32),
                pltpu.VMEM((2, N, N), F32),
                pltpu.VMEM((BATCH, 2, N, N), F32),
                pltpu.VMEM((BATCH, 2, N, N), F32),
                pltpu.VMEM((2, 2, N, N), F32),
                pltpu.VMEM((NB * BATCH, N, N), F32),
                pltpu.VMEM((2, 2, N, N), F32),
                pltpu.VMEM((2, N, N), F32),
                pltpu.VMEM((N, N), F32),
                pltpu.VMEM((2, 2, 2 * N, 2 * N), BF16),
                pltpu.SMEM((2, NB * BATCH), jnp.int32),
                pltpu.SMEM((1, 1), jnp.int32),
                pltpu.SemaphoreType.DMA((10, 2, 2)),
                pltpu.SemaphoreType.DMA((10, 2, 2)),
                pltpu.SemaphoreType.DMA((4 + NB,)),
                pltpu.SemaphoreType.DMA((4 + NB,)),
                pltpu.SemaphoreType.DMA((2,)),
                pltpu.SemaphoreType.DMA((2,)),
                pltpu.SemaphoreType.DMA((3,)),
            ],
            compiler_params=pltpu.CompilerParams(
                collective_id=0, has_side_effects=True, vmem_limit_bytes=48 * 1024 * 1024
            ),
        )(
            offsets[0, 0].T, counts, object_field, probe, propagator, intensity[0, 0], jnp.asarray(tables),
        )

    in_specs = (
        P(None, None, "gx", "gy"),
        P(),
        P(),
        P("gx", "gy", None, None),
        P("gx", "gy"),
        P("gx", "gy", None, None, None),
    )
    out_specs = P(None, None, "gx", "gy")
    return jax.shard_map(local, mesh=mesh, in_specs=in_specs, out_specs=out_specs, check_vma=False)
```

```python
import math

import jax
import jax.numpy as jnp
import ml_dtypes
import numpy as np
from jax import lax
from jax.experimental import pallas as pl
from jax.experimental.pallas import tpu as pltpu
from jax.sharding import PartitionSpec as P

MESH = pl.DeviceIdType.MESH
N = 128
H = 64
BATCH = 2
NB = 6
STEP = 0.08
F32 = jnp.float32
BF16 = jnp.bfloat16

Y_RE, Z_IM, M_RS, Z_M, Z_RE, Y_IM = range(6)
K_YRE, K_ZIM_U, K_ZIM_D, K_M, K_ZM_U, K_ZM_D, K_ZRE_U, K_ZRE_D, K_YIM, K_P3 = range(10)
FIRST, USUAL, LAST = range(3)
ALL = pl.ds(0, 2 * N)
TOP = pl.ds(0, N)
BOT = pl.ds(N, N)


def dft_tables():
    index = np.arange(N)
    phase = (index[:, None] * index[None, :] % N) * (2.0 * math.pi / N)
    c, s = np.cos(phase) / math.sqrt(N), np.sin(phase) / math.sqrt(N)
    out = []
    for sign in (-1.0, 1.0):
        m = np.block([[c, sign * s], [-sign * s, c]])
        hi = m.astype(ml_dtypes.bfloat16)
        out.append(np.stack([hi, (m - hi.astype(np.float64)).astype(ml_dtypes.bfloat16)]))
    return np.stack(out)


def place(hi_x, lo_x, y, z, core):
    return hi_x * 4 + z, (lo_x * 4 + y) * 2 + core


def parts(gx, gy):
    return lax.div(gx, 4), lax.rem(gx, 4), lax.div(gy, 8), lax.rem(lax.div(gy, 2), 4), lax.rem(gy, 2)


def tile_of(gx, gy):
    hi_x, z, lo_x, y, core = parts(gx, gy)
    lo_x = lax.rem(lo_x + hi_x, 2)
    z = jnp.where(hi_x == 1, 3 - z, z)
    y = jnp.where(lo_x == 1, 3 - y, y)
    return place(hi_x, lo_x, y, z, core)


def device_of(gx, gy):
    hi_x, z, lo_x, y, core = parts(gx, gy)
    z = jnp.where(hi_x == 1, 3 - z, z)
    y = jnp.where(lo_x == 1, 3 - y, y)
    return place(hi_x, lax.rem(lo_x + hi_x, 2), y, z, core)


def cmul(ar, ai, br, bi):
    return ar * br - ai * bi, ar * bi + ai * br


def kernel(
    offs_in, cnt_in, obj, probe_in, prop_in, inten_in, w_in, out,
    o0, o1, d, z, r, a, q, psi, pat, tile, inten, fin, probe, prop, w, offs, cnt,
    ssem, rsem, in_send, in_recv, out_send, out_recv, lsem,
):
    objects = (o0, o1)
    me = (lax.axis_index("gx"), lax.axis_index("gy"))
    gx, gy = tile_of(*me)
    core = lax.rem(gy, 2)
    home = (gx, gy)
    worker = device_of(*me)
    moved = jnp.logical_or(gx != me[0], gy != me[1])
    stays = jnp.logical_not(moved)
    has_u = gx > 0
    has_d = gx < 7
    has_o = jnp.logical_and(gy > 0, gy < 15)
    up = device_of(jnp.maximum(gx - 1, 0), gy)
    dn = device_of(jnp.minimum(gx + 1, 7), gy)
    mate = device_of(gx, gy + 1 - 2 * core)
    outer = device_of(gx, jnp.clip(gy - 1 + 2 * core, 0, 15))
    hl = 1 - core
    hr = core

    lane = lax.broadcasted_iota(jnp.int32, (1, N), 1)
    row = lax.broadcasted_iota(jnp.int32, (2 * N, N), 0)
    row_ok = jnp.logical_and(row >= jnp.where(gx == 0, H, 0), row < jnp.where(gx == 7, 3 * H, 4 * H))
    l_ok = lane >= jnp.where(gy == 0, H, 0)
    r_ok = lane < jnp.where(gy == 15, H, N)

    def desc(kind, src, dst, s, slot, dev):
        return pltpu.make_async_remote_copy(
            src_ref=src,
            dst_ref=dst,
            send_sem=ssem.at[kind, s, slot],
            recv_sem=rsem.at[kind, s, slot],
            device_id=dev,
            device_id_type=MESH,
        )

    def up_rows(mode):
        return {FIRST: (pl.ds(H, H), pl.ds(3 * H, H)), USUAL: (TOP, BOT), LAST: (pl.ds(0, H), pl.ds(N, H))}[mode]

    def down_rows(mode):
        return {FIRST: (pl.ds(N, H), pl.ds(0, H)), USUAL: (BOT, TOP), LAST: (pl.ds(3 * H, H), pl.ds(H, H))}[mode]

    def first_rows(mode):
        return pl.ds(H, N) if mode == FIRST else ALL

    def last_rows(mode):
        return pl.ds(H, N) if mode == LAST else ALL

    def along_z(kind, src, group, s, slot, mode, upward):
        (rows, landing), dev = (up_rows(mode), up) if upward else (down_rows(mode), dn)
        return desc(kind, src.at[rows], r.at[group, s, slot, landing], s, slot, dev)

    def copy(kind, s, slot, mode):
        if kind == K_YRE:
            rows = first_rows(mode)
            plane = 0 if s == 0 else 1 - core
            return desc(kind, d.at[s, 1, plane, rows], r.at[Y_RE, s, slot, rows], s, slot, outer)
        if kind in (K_ZIM_U, K_ZIM_D):
            plane = 1 if s == 0 else 1 - core
            return along_z(kind, d.at[s, 1, plane], Z_IM, s, slot, FIRST if mode == FIRST else USUAL, kind == K_ZIM_U)
        if kind == K_M:
            rows = first_rows(mode)
            return desc(kind, d.at[s, 0, 1 - core, rows], r.at[M_RS, s, slot, rows], s, slot, mate)
        if kind in (K_ZM_U, K_ZM_D):
            return along_z(kind, a.at[2, s], Z_M, s, slot, mode, kind == K_ZM_U)
        if kind in (K_ZRE_U, K_ZRE_D):
            return along_z(kind, a.at[0, s], Z_RE, s, slot, mode, kind == K_ZRE_U)
        rows = last_rows(mode)
        if kind == K_YIM and s == 0:
            return desc(kind, a.at[1, s, rows], r.at[Y_IM, s, slot, rows], s, slot, outer)
        half, dev = (1, outer) if kind == K_YIM else (0, mate)
        return desc(kind, objects[s].at[half, core, rows], objects[s].at[half, core, rows], s, slot, dev)

    def landed(kind, s, slot, mode):
        if kind == K_P3 or (kind == K_YIM and s == 1):
            rows = last_rows(mode)
            half, dev = (1, outer) if kind == K_YIM else (0, mate)
            return desc(kind, objects[s].at[half, core, rows], objects[s].at[half, 1 - core, rows], s, slot, dev)
        return copy(kind, s, slot, mode)

    def both_of(x, y):
        return jnp.logical_and(x, y)

    has_no = jnp.logical_not(has_o)
    senders = [
        {K_YRE: has_o, K_ZIM_U: has_u, K_ZIM_D: has_d, K_M: None, K_ZM_U: has_u, K_ZM_D: has_d,
         K_ZRE_U: has_u, K_ZRE_D: has_d, K_YIM: has_o, K_P3: None},
    ]
    senders.append({**senders[0], K_ZIM_U: both_of(has_u, has_no), K_ZIM_D: both_of(has_d, has_no)})
    other_way = {K_ZIM_U: K_ZIM_D, K_ZM_U: K_ZM_D, K_ZRE_U: K_ZRE_D}
    other_way.update({v: k for k, v in other_way.items()})

    def guarded(cond, fn):
        if cond is None:
            fn()
        else:
            pl.when(cond)(fn)

    def send(kind, s, slot, mode):
        guarded(senders[s][kind], lambda: copy(kind, s, slot, mode).start())

    def recv(kind, s, slot, mode):
        guarded(senders[s][other_way.get(kind, kind)], lambda: landed(kind, s, slot, mode).wait_recv())

    def sent(kind, s, slot, mode):
        guarded(senders[s][kind], lambda: copy(kind, s, slot, mode).wait_send())

    def start(s, slot, mode):
        send(K_M, s, slot, mode)
        send(K_YRE, s, slot, mode)
        send(K_ZIM_U, s, slot, mode)
        send(K_ZIM_D, s, slot, mode)

    def mid_m(s, slot, mode):
        recv(K_M, s, slot, mode)
        a[2, s] = d[s, 0, core] + r[M_RS, s, slot]
        send(K_ZM_U, s, slot, mode)
        send(K_ZM_D, s, slot, mode)

    def mid_re(s, slot, mode):
        recv(K_YRE, s, slot, mode)
        a[0, s] = d[s, 1, 0 if s == 0 else core] + r[Y_RE, s, slot]
        send(K_ZRE_U, s, slot, mode)
        send(K_ZRE_D, s, slot, mode)

    def mid_im(slot, mode):
        recv(K_ZIM_U, 0, slot, mode)
        recv(K_ZIM_D, 0, slot, mode)
        a[1, 0] = d[0, 1, 1] + r[Z_IM, 0, slot]
        send(K_YIM, 0, slot, mode)

    def mid_back(s, slot, mode):
        recv(K_ZM_U, s, slot, mode)
        recv(K_ZM_D, s, slot, mode)
        objects[s][0, core] = objects[s][0, core] + (a[2, s] + r[Z_M, s, slot])
        send(K_P3, s, slot, mode)

    def outer_back(slot, mode):
        recv(K_ZRE_U, 1, slot, mode)
        recv(K_ZRE_D, 1, slot, mode)
        o1[1, core] = o1[1, core] + (a[0, 1] + r[Z_RE, 1, slot])
        send(K_YIM, 1, slot, mode)
        recv(K_ZIM_U, 1, slot, mode)
        recv(K_ZIM_D, 1, slot, mode)

        @pl.when(has_no)
        def _():
            o1[1, 1 - core] = o1[1, 1 - core] + (d[1, 1, 1 - core] + r[Z_IM, 1, slot])

    def finish_0(slot, mode):
        recv(K_ZRE_U, 0, slot, mode)
        recv(K_ZRE_D, 0, slot, mode)
        o0[1, 0] = o0[1, 0] + (a[0, 0] + r[Z_RE, 0, slot])
        recv(K_YIM, 0, slot, mode)
        o0[1, 1] = o0[1, 1] + (a[1, 0] + r[Y_IM, 0, slot])
        recv(K_P3, 0, slot, mode)
        for kind in range(10):
            sent(kind, 0, slot, mode)

    def drain_1(slot, mode):
        for kind in range(8):
            sent(kind, 1, slot, mode)

    def finish_1(slot, mode):
        for kind in (K_P3, K_YIM):
            recv(kind, 1, slot, mode)
            sent(kind, 1, slot, mode)

    def exchange(slot, mode):
        mid_m(1, slot, mode)
        mid_m(0, slot, mode)
        mid_re(1, slot, mode)
        mid_re(0, slot, mode)
        mid_im(slot, mode)
        mid_back(1, slot, mode)
        mid_back(0, slot, mode)
        outer_back(slot, mode)
        drain_1(slot, mode)
        if mode == LAST:
            finish_1(slot, mode)
            give(1)
        finish_0(slot, mode)

    def send_home(s):
        return pltpu.make_async_remote_copy(
            src_ref=fin.at[s],
            dst_ref=out.at[s],
            send_sem=out_send.at[s],
            recv_sem=out_recv.at[s],
            device_id=home,
            device_id_type=MESH,
        )

    def give(s):
        for c in range(2):
            left = objects[s][hl, c, pl.ds(H, N), :]
            right = objects[s][hr, c, pl.ds(H, N), :]
            fin[s, c] = pltpu.roll(jnp.where(lane >= H, left, right), H, 1)
        pl.when(moved)(lambda: send_home(s).start())

        @pl.when(stays)
        def _():
            out[s] = fin[s]

    inputs = [(offs_in, offs), (cnt_in, cnt)]
    inputs += [(obj.at[s], tile.at[s]) for s in range(2)]

    def pass_on(i, src, dst):
        return pltpu.make_async_remote_copy(
            src_ref=src,
            dst_ref=dst,
            send_sem=in_send.at[i],
            recv_sem=in_recv.at[i],
            device_id=worker,
            device_id_type=MESH,
        )

    def keep(i, src, dst):
        return pltpu.make_async_copy(src, dst, in_send.at[i])

    def pass_start(i, src, dst):
        pl.when(moved)(lambda: pass_on(i, src, dst).start())
        pl.when(stays)(lambda: keep(i, src, dst).start())

    def pass_wait(i, src, dst):
        @pl.when(moved)
        def _():
            pass_on(i, src, dst).wait_send()
            pass_on(i, src, dst).wait_recv()

        pl.when(stays)(lambda: keep(i, src, dst).wait())

    def frames(b):
        return 4 + b, inten_in.at[pl.ds(BATCH * b, BATCH)], inten.at[pl.ds(BATCH * b, BATCH)]

    consts = [(probe_in, probe), (prop_in, prop), (w_in, w)]
    barrier = pltpu.get_barrier_semaphore()
    greet = ((None, mate), (has_u, up), (has_d, dn), (has_o, outer), (moved, home), (moved, worker))
    for cond, dev in greet:
        guarded(cond, lambda dev=dev: pl.semaphore_signal(barrier, inc=1, device_id=dev, device_id_type=MESH))
    for i, (src, dst) in enumerate(consts):
        pltpu.make_async_copy(src, dst, lsem.at[i]).start()
    count = 1 + sum(jnp.where(cond, 1, 0) for cond, _ in greet[1:])
    pl.semaphore_wait(barrier, count)
    for i in (2, 0, 1):
        pass_start(i, *inputs[i])
    for o in objects:
        o[...] = jnp.zeros_like(o)
    d[...] = jnp.zeros_like(d)
    z[...] = jnp.zeros_like(z)
    for group, rows in ((Y_RE, ((0, H), (3 * H, H))), (M_RS, ((0, H), (3 * H, H)))):
        for first, n in rows:
            r[group, :, 0, pl.ds(first, n)] = jnp.zeros((2, n, N), F32)
    for group in (Z_IM, Z_M, Z_RE):
        r[group, :, 0, pl.ds(H, N)] = jnp.zeros((2, N, N), F32)

    @pl.when(gx == 0)
    def _():
        for group in (Z_IM, Z_M, Z_RE):
            r[group, :, :, TOP] = jnp.zeros((2, 2, N, N), F32)

    @pl.when(gx == 7)
    def _():
        for group in (Z_IM, Z_M, Z_RE):
            r[group, :, :, BOT] = jnp.zeros((2, 2, N, N), F32)

    @pl.when(has_no)
    def _():
        for group in (Y_RE, Y_IM):
            r[group] = jnp.zeros((2, 2, 2 * N, N), F32)

    for i, (src, dst) in enumerate(consts):
        pltpu.make_async_copy(src, dst, lsem.at[i]).wait()
    q[0] = jnp.cos(prop[...])
    q[1] = jnp.sin(prop[...])
    pass_start(3, *inputs[3])

    for s in (0, 1):
        pass_wait(2 + s, *inputs[2 + s])
        if s == 1:
            pass_start(*frames(0))
        for c in range(2):
            cells = pltpu.roll(tile[s, c], H, 1)
            d[s, hl, c, pl.ds(H, N)] = jnp.where(lane >= H, cells, 0.0)
            d[s, hr, c, pl.ds(H, N)] = jnp.where(lane < H, cells, 0.0)
        start(s, 0, FIRST)
    for i in range(2):
        pass_wait(i, *inputs[i])
    exchange(0, FIRST)

    def split(x):
        hi = x.astype(BF16)
        return hi, (x - hi.astype(F32)).astype(BF16)

    def transform(re, im, inverse):
        x = jnp.concatenate([jnp.concatenate([re[m], im[m]], 1) for m in range(BATCH)], 0)
        hi, lo = split(x)
        right = jnp.concatenate([w[inverse, 0], w[inverse, 0], w[inverse, 1]], 0)
        y = jnp.dot(jnp.concatenate([hi, lo, hi], 1), right, preferred_element_type=F32)
        x = jnp.concatenate(
            [jnp.concatenate([y[:N, :N], y[N:, :N]], 1), jnp.concatenate([y[:N, N:], y[N:, N:]], 1)], 0
        )
        hi, lo = split(x)
        left = jnp.concatenate([w[1 - inverse, 0], w[1 - inverse, 0], w[1 - inverse, 1]], 1)
        y = jnp.dot(left, jnp.concatenate([hi, lo, hi], 0), preferred_element_type=F32)
        return (y[:N, :N], y[:N, N:]), (y[N:, :N], y[N:, N:])

    def patch(s, c, r0, q0):
        left = objects[s][hl, c, pl.ds(r0, N), :]
        right = objects[s][hr, c, pl.ds(r0, N), :]
        return pltpu.roll(jnp.where(lane >= q0, left, right), (N - q0) & (N - 1), 1)

    def scatter(s, places, grads):
        for m in range(BATCH):
            r0, q0, weight = places[m]
            fl = jnp.where(jnp.logical_and(lane >= q0, l_ok), weight, 0.0)
            fr = jnp.where(jnp.logical_and(lane < q0, r_ok), weight, 0.0)
            for c in range(2):
                g = pltpu.roll(grads[c][m], q0 & (N - 1), 1)
                z[m, 0, c, pl.ds(N, N)] = g * fl
                z[m, 1, c, pl.ds(N, N)] = g * fr
        for h, half in ((0, hl), (1, hr)):
            for c in range(2):
                total = z[0, h, c, pl.ds(N - places[0][0], 2 * N), :] + z[1, h, c, pl.ds(N - places[1][0], 2 * N), :]
                d[s, half, c] = jnp.where(row_ok, total, 0.0)

    def batch(b, carry):
        slot = lax.rem(b + 1, 2)
        before = lax.rem(b, 2)
        pl.when(b < NB - 1)(lambda: pass_start(*frames(b + 1)))
        places = []
        for m in range(BATCH):
            n = b * BATCH + m
            weight = jnp.where(n < cnt[0, 0], -STEP, 0.0).astype(F32)
            places.append((offs[0, n], offs[1, n], weight))
        pr, pi = probe[0], probe[1]
        re, im = [], []
        for m in range(BATCH):
            r0, q0, _ = places[m]
            x, y = cmul(pr, pi, patch(0, 0, r0, q0), patch(0, 1, r0, q0))
            re.append(x)
            im.append(y)
        re, im = transform(re, im, 0)
        both = [cmul(re[m], im[m], q[0], q[1]) for m in range(BATCH)]
        re, im = transform([x for x, _ in both], [y for _, y in both], 1)
        for m in range(BATCH):
            psi[m, 0] = re[m]
            psi[m, 1] = im[m]
        finish_1(before, USUAL)
        both = []
        for m in range(BATCH):
            r0, q0, _ = places[m]
            for c in range(2):
                pat[m, c] = patch(1, c, r0, q0)
            both.append(cmul(psi[m, 0], psi[m, 1], pat[m, 0], pat[m, 1]))
        re, im = transform([x for x, _ in both], [y for _, y in both], 0)
        pass_wait(*frames(b))
        excess = [re[m] * re[m] + im[m] * im[m] - inten[b * BATCH + m] for m in range(BATCH)]
        re, im = transform([excess[m] * re[m] for m in range(BATCH)], [excess[m] * im[m] for m in range(BATCH)], 1)
        both = [cmul(psi[m, 0], -psi[m, 1], re[m], im[m]) for m in range(BATCH)]
        scatter(1, places, ([x for x, _ in both], [y for _, y in both]))
        start(1, slot, USUAL)
        both = [cmul(pat[m, 0], -pat[m, 1], re[m], im[m]) for m in range(BATCH)]
        re, im = transform([x for x, _ in both], [y for _, y in both], 0)
        both = [cmul(re[m], im[m], q[0], -q[1]) for m in range(BATCH)]
        re, im = transform([x for x, _ in both], [y for _, y in both], 1)
        both = [cmul(re[m], im[m], pr, -pi) for m in range(BATCH)]
        scatter(0, places, ([x for x, _ in both], [y for _, y in both]))
        start(0, slot, USUAL)
        pl.when(b < NB - 1)(lambda: exchange(slot, USUAL))
        pl.when(b == NB - 1)(lambda: exchange(slot, LAST))
        return carry

    lax.fori_loop(0, NB, batch, 0)
    give(0)
    for s in range(2):
        @pl.when(moved)
        def _():
            send_home(s).wait_send()
            send_home(s).wait_recv()


def solution(mesh):
    tables = dft_tables()

    def local(object_field, probe, propagator, offsets, counts, intensity):
        hbm = pl.BlockSpec(memory_space=pltpu.HBM)
        return pl.pallas_call(
            kernel,
            out_shape=jax.ShapeDtypeStruct((2, 2, N, N), F32),
            in_specs=[hbm] * 7,
            out_specs=pl.BlockSpec(memory_space=pltpu.VMEM),
            scratch_shapes=[
                pltpu.VMEM((2, 2, 2 * N, N), F32),
                pltpu.VMEM((2, 2, 2 * N, N), F32),
                pltpu.VMEM((2, 2, 2, 2 * N, N), F32),
                pltpu.VMEM((BATCH, 2, 2, 3 * N, N), F32),
                pltpu.VMEM((6, 2, 2, 2 * N, N), F32),
                pltpu.VMEM((3, 2, 2 * N, N), F32),
                pltpu.VMEM((2, N, N), F32),
                pltpu.VMEM((BATCH, 2, N, N), F32),
                pltpu.VMEM((BATCH, 2, N, N), F32),
                pltpu.VMEM((2, 2, N, N), F32),
                pltpu.VMEM((NB * BATCH, N, N), F32),
                pltpu.VMEM((2, 2, N, N), F32),
                pltpu.VMEM((2, N, N), F32),
                pltpu.VMEM((N, N), F32),
                pltpu.VMEM((2, 2, 2 * N, 2 * N), BF16),
                pltpu.SMEM((2, NB * BATCH), jnp.int32),
                pltpu.SMEM((1, 1), jnp.int32),
                pltpu.SemaphoreType.DMA((10, 2, 2)),
                pltpu.SemaphoreType.DMA((10, 2, 2)),
                pltpu.SemaphoreType.DMA((4 + NB,)),
                pltpu.SemaphoreType.DMA((4 + NB,)),
                pltpu.SemaphoreType.DMA((2,)),
                pltpu.SemaphoreType.DMA((2,)),
                pltpu.SemaphoreType.DMA((3,)),
            ],
            compiler_params=pltpu.CompilerParams(
                collective_id=0, has_side_effects=True, vmem_limit_bytes=58 * 1024 * 1024
            ),
        )(
            offsets[0, 0].T, counts, object_field, probe, propagator, intensity[0, 0], jnp.asarray(tables),
        )

    in_specs = (
        P(None, None, "gx", "gy"),
        P(),
        P(),
        P("gx", "gy", None, None),
        P("gx", "gy"),
        P("gx", "gy", None, None, None),
    )
    out_specs = P(None, None, "gx", "gy")
    return jax.shard_map(local, mesh=mesh, in_specs=in_specs, out_specs=out_specs, check_vma=False)
```

```python
import math

import jax
import jax.numpy as jnp
import ml_dtypes
import numpy as np
from jax import lax
from jax.experimental import pallas as pl
from jax.experimental.pallas import tpu as pltpu
from jax.sharding import PartitionSpec as P

MESH = pl.DeviceIdType.MESH
N = 128
H = 64
BATCH = 2
NB = 6
STEP = 0.08
F32 = jnp.float32
BF16 = jnp.bfloat16

Y_RE, Z_IM, M_RS, Z_M, Z_RE, Y_IM = range(6)
K_YRE, K_ZIM_U, K_ZIM_D, K_M, K_ZM_U, K_ZM_D, K_ZRE_U, K_ZRE_D, K_YIM, K_P3 = range(10)
FIRST, USUAL, LAST = range(3)
ALL = pl.ds(0, 2 * N)
TOP = pl.ds(0, N)
BOT = pl.ds(N, N)


def dft_tables():
    index = np.arange(N)
    phase = (index[:, None] * index[None, :] % N) * (2.0 * math.pi / N)
    c, s = np.cos(phase) / math.sqrt(N), np.sin(phase) / math.sqrt(N)
    out = []
    for sign in (-1.0, 1.0):
        m = np.block([[c, sign * s], [-sign * s, c]])
        hi = m.astype(ml_dtypes.bfloat16)
        out.append(np.stack([hi, (m - hi.astype(np.float64)).astype(ml_dtypes.bfloat16)]))
    return np.stack(out)


def place(hi_x, lo_x, y, z, core):
    return hi_x * 4 + z, (lo_x * 4 + y) * 2 + core


def parts(gx, gy):
    return lax.div(gx, 4), lax.rem(gx, 4), lax.div(gy, 8), lax.rem(lax.div(gy, 2), 4), lax.rem(gy, 2)


def tile_of(gx, gy):
    hi_x, z, lo_x, y, core = parts(gx, gy)
    lo_x = lax.rem(lo_x + hi_x, 2)
    z = jnp.where(hi_x == 0, 3 - z, z)
    y = jnp.where(lo_x == 1, 3 - y, y)
    return place(hi_x, lo_x, y, z, core)


def device_of(gx, gy):
    hi_x, z, lo_x, y, core = parts(gx, gy)
    z = jnp.where(hi_x == 0, 3 - z, z)
    y = jnp.where(lo_x == 1, 3 - y, y)
    return place(hi_x, lax.rem(lo_x + hi_x, 2), y, z, core)


def cmul(ar, ai, br, bi):
    return ar * br - ai * bi, ar * bi + ai * br


def kernel(
    offs_in, cnt_in, obj, probe_in, prop_in, inten_in, w_in, out,
    o0, o1, d, z, r, a, q, psi, pat, tile, inten, fin, probe, prop, w, offs, cnt,
    ssem, rsem, in_send, in_recv, out_send, out_recv, lsem,
):
    objects = (o0, o1)
    me = (lax.axis_index("gx"), lax.axis_index("gy"))
    gx, gy = tile_of(*me)
    core = lax.rem(gy, 2)
    home = (gx, gy)
    worker = device_of(*me)
    moved = jnp.logical_or(gx != me[0], gy != me[1])
    stays = jnp.logical_not(moved)
    has_u = gx > 0
    has_d = gx < 7
    has_o = jnp.logical_and(gy > 0, gy < 15)
    up = device_of(jnp.maximum(gx - 1, 0), gy)
    dn = device_of(jnp.minimum(gx + 1, 7), gy)
    mate = device_of(gx, gy + 1 - 2 * core)
    outer = device_of(gx, jnp.clip(gy - 1 + 2 * core, 0, 15))
    hl = 1 - core
    hr = core

    lane = lax.broadcasted_iota(jnp.int32, (1, N), 1)
    row = lax.broadcasted_iota(jnp.int32, (2 * N, N), 0)
    row_ok = jnp.logical_and(row >= jnp.where(gx == 0, H, 0), row < jnp.where(gx == 7, 3 * H, 4 * H))
    l_ok = lane >= jnp.where(gy == 0, H, 0)
    r_ok = lane < jnp.where(gy == 15, H, N)

    def desc(kind, src, dst, s, slot, dev):
        return pltpu.make_async_remote_copy(
            src_ref=src,
            dst_ref=dst,
            send_sem=ssem.at[kind, s, slot],
            recv_sem=rsem.at[kind, s, slot],
            device_id=dev,
            device_id_type=MESH,
        )

    def up_rows(mode):
        return {FIRST: (pl.ds(H, H), pl.ds(3 * H, H)), USUAL: (TOP, BOT), LAST: (pl.ds(0, H), pl.ds(N, H))}[mode]

    def down_rows(mode):
        return {FIRST: (pl.ds(N, H), pl.ds(0, H)), USUAL: (BOT, TOP), LAST: (pl.ds(3 * H, H), pl.ds(H, H))}[mode]

    def first_rows(mode):
        return pl.ds(H, N) if mode == FIRST else ALL

    def last_rows(mode):
        return pl.ds(H, N) if mode == LAST else ALL

    def along_z(kind, src, group, s, slot, mode, upward):
        (rows, landing), dev = (up_rows(mode), up) if upward else (down_rows(mode), dn)
        return desc(kind, src.at[rows], r.at[group, s, slot, landing], s, slot, dev)

    def copy(kind, s, slot, mode):
        if kind == K_YRE:
            rows = first_rows(mode)
            return desc(kind, d.at[s, 1, 0, rows], r.at[Y_RE, s, slot, rows], s, slot, outer)
        if kind in (K_ZIM_U, K_ZIM_D):
            return along_z(kind, d.at[s, 1, 1], Z_IM, s, slot, FIRST if mode == FIRST else USUAL, kind == K_ZIM_U)
        if kind == K_M:
            rows = first_rows(mode)
            return desc(kind, d.at[s, 0, 1 - core, rows], r.at[M_RS, s, slot, rows], s, slot, mate)
        if kind in (K_ZM_U, K_ZM_D):
            early = s == 1 and mode == LAST
            return along_z(kind, a.at[2, s], Z_M, s, slot, USUAL if early else mode, kind == K_ZM_U)
        if kind in (K_ZRE_U, K_ZRE_D):
            return along_z(kind, a.at[0, s], Z_RE, s, slot, mode, kind == K_ZRE_U)
        rows = last_rows(mode)
        if kind == K_YIM:
            return desc(kind, a.at[1, s, rows], r.at[Y_IM, s, slot, rows], s, slot, outer)
        return desc(kind, objects[s].at[0, core, rows], objects[s].at[0, core, rows], s, slot, mate)

    def landed(kind, s, slot, mode):
        if kind == K_P3:
            rows = last_rows(mode)
            return desc(kind, objects[s].at[0, core, rows], objects[s].at[0, 1 - core, rows], s, slot, mate)
        return copy(kind, s, slot, mode)

    has_no = jnp.logical_not(has_o)
    senders = {
        K_YRE: has_o, K_ZIM_U: has_u, K_ZIM_D: has_d, K_M: None, K_ZM_U: has_u, K_ZM_D: has_d,
        K_ZRE_U: has_u, K_ZRE_D: has_d, K_YIM: has_o, K_P3: None,
    }
    other_way = {K_ZIM_U: K_ZIM_D, K_ZM_U: K_ZM_D, K_ZRE_U: K_ZRE_D}
    other_way.update({v: k for k, v in other_way.items()})

    def guarded(cond, fn):
        if cond is None:
            fn()
        else:
            pl.when(cond)(fn)

    def send(kind, s, slot, mode):
        guarded(senders[kind], lambda: copy(kind, s, slot, mode).start())

    def recv(kind, s, slot, mode):
        guarded(senders[other_way.get(kind, kind)], lambda: landed(kind, s, slot, mode).wait_recv())

    def sent(kind, s, slot, mode):
        guarded(senders[kind], lambda: copy(kind, s, slot, mode).wait_send())

    def start(s, slot, mode):
        send(K_M, s, slot, mode)
        send(K_YRE, s, slot, mode)
        send(K_ZIM_U, s, slot, mode)
        send(K_ZIM_D, s, slot, mode)

    def mid_m(s, slot, mode):
        recv(K_M, s, slot, mode)
        a[2, s] = d[s, 0, core] + r[M_RS, s, slot]
        send(K_ZM_U, s, slot, mode)
        send(K_ZM_D, s, slot, mode)

    def mid_re(s, slot, mode):
        recv(K_YRE, s, slot, mode)
        a[0, s] = d[s, 1, 0] + r[Y_RE, s, slot]
        send(K_ZRE_U, s, slot, mode)
        send(K_ZRE_D, s, slot, mode)

    def mid_im(s, slot, mode):
        recv(K_ZIM_U, s, slot, mode)
        recv(K_ZIM_D, s, slot, mode)
        a[1, s] = d[s, 1, 1] + r[Z_IM, s, slot]
        send(K_YIM, s, slot, mode)

    def mid_back(s, slot, mode):
        recv(K_ZM_U, s, slot, mode)
        recv(K_ZM_D, s, slot, mode)
        objects[s][0, core] = objects[s][0, core] + (a[2, s] + r[Z_M, s, slot])
        send(K_P3, s, slot, mode)

    def finish(s, slot, mode):
        recv(K_ZRE_U, s, slot, mode)
        recv(K_ZRE_D, s, slot, mode)
        objects[s][1, 0] = objects[s][1, 0] + (a[0, s] + r[Z_RE, s, slot])
        recv(K_YIM, s, slot, mode)
        objects[s][1, 1] = objects[s][1, 1] + (a[1, s] + r[Y_IM, s, slot])
        recv(K_P3, s, slot, mode)
        for kind in range(10):
            sent(kind, s, slot, mode)

    def exchange(slot, mode):
        mid_m(0, slot, mode)
        mid_re(1, slot, mode)
        mid_im(1, slot, mode)
        mid_re(0, slot, mode)
        mid_im(0, slot, mode)
        mid_back(1, slot, mode)
        mid_back(0, slot, mode)
        if mode == LAST:
            finish(1, slot, mode)
            give(1)
        finish(0, slot, mode)

    def send_home(s):
        return pltpu.make_async_remote_copy(
            src_ref=fin.at[s],
            dst_ref=out.at[s],
            send_sem=out_send.at[s],
            recv_sem=out_recv.at[s],
            device_id=home,
            device_id_type=MESH,
        )

    def give(s):
        for c in range(2):
            left = objects[s][hl, c, pl.ds(H, N), :]
            right = objects[s][hr, c, pl.ds(H, N), :]
            fin[s, c] = pltpu.roll(jnp.where(lane >= H, left, right), H, 1)
        pl.when(moved)(lambda: send_home(s).start())

        @pl.when(stays)
        def _():
            out[s] = fin[s]

    inputs = [(offs_in, offs), (cnt_in, cnt)]
    inputs += [(obj.at[s], tile.at[s]) for s in range(2)]

    def pass_on(i, src, dst):
        return pltpu.make_async_remote_copy(
            src_ref=src,
            dst_ref=dst,
            send_sem=in_send.at[i],
            recv_sem=in_recv.at[i],
            device_id=worker,
            device_id_type=MESH,
        )

    def keep(i, src, dst):
        return pltpu.make_async_copy(src, dst, in_send.at[i])

    def pass_start(i, src, dst):
        pl.when(moved)(lambda: pass_on(i, src, dst).start())
        pl.when(stays)(lambda: keep(i, src, dst).start())

    def pass_wait(i, src, dst):
        @pl.when(moved)
        def _():
            pass_on(i, src, dst).wait_send()
            pass_on(i, src, dst).wait_recv()

        pl.when(stays)(lambda: keep(i, src, dst).wait())

    def frames(b):
        return 4 + b, inten_in.at[pl.ds(BATCH * b, BATCH)], inten.at[pl.ds(BATCH * b, BATCH)]

    consts = [(probe_in, probe), (prop_in, prop), (w_in, w)]
    barrier = pltpu.get_barrier_semaphore()
    greet = ((None, mate), (has_u, up), (has_d, dn), (has_o, outer), (moved, home), (moved, worker))
    for cond, dev in greet:
        guarded(cond, lambda dev=dev: pl.semaphore_signal(barrier, inc=1, device_id=dev, device_id_type=MESH))
    for i, (src, dst) in enumerate(consts):
        pltpu.make_async_copy(src, dst, lsem.at[i]).start()
    count = 1 + sum(jnp.where(cond, 1, 0) for cond, _ in greet[1:])
    pl.semaphore_wait(barrier, count)
    for i in (2, 0, 1):
        pass_start(i, *inputs[i])
    for o in objects:
        o[...] = jnp.zeros_like(o)
    d[...] = jnp.zeros_like(d)
    z[...] = jnp.zeros_like(z)
    for group, rows in ((Y_RE, ((0, H), (3 * H, H))), (M_RS, ((0, H), (3 * H, H)))):
        for first, n in rows:
            r[group, :, 0, pl.ds(first, n)] = jnp.zeros((2, n, N), F32)
    for group in (Z_IM, Z_M, Z_RE):
        r[group, :, 0, pl.ds(H, N)] = jnp.zeros((2, N, N), F32)

    @pl.when(gx == 0)
    def _():
        for group in (Z_IM, Z_M, Z_RE):
            r[group, :, :, TOP] = jnp.zeros((2, 2, N, N), F32)

    @pl.when(gx == 7)
    def _():
        for group in (Z_IM, Z_M, Z_RE):
            r[group, :, :, BOT] = jnp.zeros((2, 2, N, N), F32)

    @pl.when(has_no)
    def _():
        for group in (Y_RE, Y_IM):
            r[group] = jnp.zeros((2, 2, 2 * N, N), F32)

    for i, (src, dst) in enumerate(consts):
        pltpu.make_async_copy(src, dst, lsem.at[i]).wait()
    q[0] = jnp.cos(prop[...])
    q[1] = jnp.sin(prop[...])
    pass_start(3, *inputs[3])

    def begin(s):
        pass_wait(2 + s, *inputs[2 + s])
        for c in range(2):
            cells = pltpu.roll(tile[s, c], H, 1)
            d[s, hl, c, pl.ds(H, N)] = jnp.where(lane >= H, cells, 0.0)
            d[s, hr, c, pl.ds(H, N)] = jnp.where(lane < H, cells, 0.0)
        start(s, 0, FIRST)

    begin(0)
    mid_m(0, 0, FIRST)
    begin(1)
    pass_start(*frames(0))
    mid_re(0, 0, FIRST)
    mid_im(0, 0, FIRST)
    mid_m(1, 0, FIRST)
    mid_back(0, 0, FIRST)
    mid_re(1, 0, FIRST)
    mid_im(1, 0, FIRST)
    mid_back(1, 0, FIRST)
    for i in range(2):
        pass_wait(i, *inputs[i])
    finish(0, 0, FIRST)

    def split(x):
        hi = x.astype(BF16)
        return hi, (x - hi.astype(F32)).astype(BF16)

    def transform(re, im, inverse):
        x = jnp.concatenate([jnp.concatenate([re[m], im[m]], 1) for m in range(BATCH)], 0)
        hi, lo = split(x)
        right = jnp.concatenate([w[inverse, 0], w[inverse, 0], w[inverse, 1]], 0)
        y = jnp.dot(jnp.concatenate([hi, lo, hi], 1), right, preferred_element_type=F32)
        x = jnp.concatenate(
            [jnp.concatenate([y[:N, :N], y[N:, :N]], 1), jnp.concatenate([y[:N, N:], y[N:, N:]], 1)], 0
        )
        hi, lo = split(x)
        left = jnp.concatenate([w[1 - inverse, 0], w[1 - inverse, 0], w[1 - inverse, 1]], 1)
        y = jnp.dot(left, jnp.concatenate([hi, lo, hi], 0), preferred_element_type=F32)
        return (y[:N, :N], y[:N, N:]), (y[N:, :N], y[N:, N:])

    def patch(s, c, r0, q0):
        left = objects[s][hl, c, pl.ds(r0, N), :]
        right = objects[s][hr, c, pl.ds(r0, N), :]
        return pltpu.roll(jnp.where(lane >= q0, left, right), (N - q0) & (N - 1), 1)

    def scatter(s, places, grads):
        for m in range(BATCH):
            r0, q0, weight = places[m]
            fl = jnp.where(jnp.logical_and(lane >= q0, l_ok), weight, 0.0)
            fr = jnp.where(jnp.logical_and(lane < q0, r_ok), weight, 0.0)
            for c in range(2):
                g = pltpu.roll(grads[c][m], q0 & (N - 1), 1)
                z[m, 0, c, pl.ds(N, N)] = g * fl
                z[m, 1, c, pl.ds(N, N)] = g * fr
        for h, half in ((0, hl), (1, hr)):
            for c in range(2):
                total = z[0, h, c, pl.ds(N - places[0][0], 2 * N), :] + z[1, h, c, pl.ds(N - places[1][0], 2 * N), :]
                d[s, half, c] = jnp.where(row_ok, total, 0.0)

    def batch(b, carry):
        slot = lax.rem(b + 1, 2)
        before = lax.rem(b, 2)
        pl.when(b < NB - 1)(lambda: pass_start(*frames(b + 1)))
        places = []
        for m in range(BATCH):
            n = b * BATCH + m
            weight = jnp.where(n < cnt[0, 0], -STEP, 0.0).astype(F32)
            places.append((offs[0, n], offs[1, n], weight))
        pr, pi = probe[0], probe[1]
        re, im = [], []
        for m in range(BATCH):
            r0, q0, _ = places[m]
            x, y = cmul(pr, pi, patch(0, 0, r0, q0), patch(0, 1, r0, q0))
            re.append(x)
            im.append(y)
        re, im = transform(re, im, 0)
        both = [cmul(re[m], im[m], q[0], q[1]) for m in range(BATCH)]
        re, im = transform([x for x, _ in both], [y for _, y in both], 1)
        for m in range(BATCH):
            psi[m, 0] = re[m]
            psi[m, 1] = im[m]
        pl.when(b == 0)(lambda: finish(1, before, FIRST))
        pl.when(b > 0)(lambda: finish(1, before, USUAL))
        both = []
        for m in range(BATCH):
            r0, q0, _ = places[m]
            for c in range(2):
                pat[m, c] = patch(1, c, r0, q0)
            both.append(cmul(psi[m, 0], psi[m, 1], pat[m, 0], pat[m, 1]))
        re, im = transform([x for x, _ in both], [y for _, y in both], 0)
        pass_wait(*frames(b))
        excess = [re[m] * re[m] + im[m] * im[m] - inten[b * BATCH + m] for m in range(BATCH)]
        re, im = transform([excess[m] * re[m] for m in range(BATCH)], [excess[m] * im[m] for m in range(BATCH)], 1)
        both = [cmul(psi[m, 0], -psi[m, 1], re[m], im[m]) for m in range(BATCH)]
        scatter(1, places, ([x for x, _ in both], [y for _, y in both]))
        start(1, slot, USUAL)
        both = [cmul(pat[m, 0], -pat[m, 1], re[m], im[m]) for m in range(BATCH)]
        re, im = transform([x for x, _ in both], [y for _, y in both], 0)
        both = [cmul(re[m], im[m], q[0], -q[1]) for m in range(BATCH)]
        re, im = transform([x for x, _ in both], [y for _, y in both], 1)
        both = [cmul(re[m], im[m], pr, -pi) for m in range(BATCH)]
        scatter(0, places, ([x for x, _ in both], [y for _, y in both]))
        start(0, slot, USUAL)
        mid_m(1, slot, USUAL)
        pl.when(b < NB - 1)(lambda: exchange(slot, USUAL))
        pl.when(b == NB - 1)(lambda: exchange(slot, LAST))
        return carry

    lax.fori_loop(0, NB, batch, 0)
    give(0)
    for s in range(2):
        @pl.when(moved)
        def _():
            send_home(s).wait_send()
            send_home(s).wait_recv()


def solution(mesh):
    tables = dft_tables()

    def local(object_field, probe, propagator, offsets, counts, intensity):
        hbm = pl.BlockSpec(memory_space=pltpu.HBM)
        return pl.pallas_call(
            kernel,
            out_shape=jax.ShapeDtypeStruct((2, 2, N, N), F32),
            in_specs=[hbm] * 7,
            out_specs=pl.BlockSpec(memory_space=pltpu.VMEM),
            scratch_shapes=[
                pltpu.VMEM((2, 2, 2 * N, N), F32),
                pltpu.VMEM((2, 2, 2 * N, N), F32),
                pltpu.VMEM((2, 2, 2, 2 * N, N), F32),
                pltpu.VMEM((BATCH, 2, 2, 3 * N, N), F32),
                pltpu.VMEM((6, 2, 2, 2 * N, N), F32),
                pltpu.VMEM((3, 2, 2 * N, N), F32),
                pltpu.VMEM((2, N, N), F32),
                pltpu.VMEM((BATCH, 2, N, N), F32),
                pltpu.VMEM((BATCH, 2, N, N), F32),
                pltpu.VMEM((2, 2, N, N), F32),
                pltpu.VMEM((NB * BATCH, N, N), F32),
                pltpu.VMEM((2, 2, N, N), F32),
                pltpu.VMEM((2, N, N), F32),
                pltpu.VMEM((N, N), F32),
                pltpu.VMEM((2, 2, 2 * N, 2 * N), BF16),
                pltpu.SMEM((2, NB * BATCH), jnp.int32),
                pltpu.SMEM((1, 1), jnp.int32),
                pltpu.SemaphoreType.DMA((10, 2, 2)),
                pltpu.SemaphoreType.DMA((10, 2, 2)),
                pltpu.SemaphoreType.DMA((4 + NB,)),
                pltpu.SemaphoreType.DMA((4 + NB,)),
                pltpu.SemaphoreType.DMA((2,)),
                pltpu.SemaphoreType.DMA((2,)),
                pltpu.SemaphoreType.DMA((3,)),
            ],
            compiler_params=pltpu.CompilerParams(
                collective_id=0, has_side_effects=True, vmem_limit_bytes=58 * 1024 * 1024
            ),
        )(
            offsets[0, 0].T, counts, object_field, probe, propagator, intensity[0, 0], jnp.asarray(tables),
        )

    in_specs = (
        P(None, None, "gx", "gy"),
        P(),
        P(),
        P("gx", "gy", None, None),
        P("gx", "gy"),
        P("gx", "gy", None, None, None),
    )
    out_specs = P(None, None, "gx", "gy")
    return jax.shard_map(local, mesh=mesh, in_specs=in_specs, out_specs=out_specs, check_vma=False)
```

```python
import math

import jax
import jax.numpy as jnp
import ml_dtypes
import numpy as np
from jax import lax
from jax.experimental import pallas as pl
from jax.experimental.pallas import tpu as pltpu
from jax.sharding import PartitionSpec as P

MESH = pl.DeviceIdType.MESH
N = 128
H = 64
BATCH = 2
NB = 6
STEP = 0.08
F32 = jnp.float32
BF16 = jnp.bfloat16

Y_RE, Z_IM, M_RS, Z_M, Z_RE, Y_IM = range(6)
K_YRE, K_ZIM_U, K_ZIM_D, K_M, K_ZM_U, K_ZM_D, K_ZRE_U, K_ZRE_D, K_YIM, K_P3 = range(10)
FIRST, USUAL, LAST = range(3)
ALL = pl.ds(0, 2 * N)
TOP = pl.ds(0, N)
BOT = pl.ds(N, N)


def dft_tables():
    index = np.arange(N)
    phase = (index[:, None] * index[None, :] % N) * (2.0 * math.pi / N)
    c, s = np.cos(phase) / math.sqrt(N), np.sin(phase) / math.sqrt(N)
    out = []
    for sign in (-1.0, 1.0):
        m = np.block([[c, sign * s], [-sign * s, c]])
        hi = m.astype(ml_dtypes.bfloat16)
        out.append(np.stack([hi, (m - hi.astype(np.float64)).astype(ml_dtypes.bfloat16)]))
    return np.stack(out)


def place(hi_x, lo_x, y, z, core):
    return hi_x * 4 + z, (lo_x * 4 + y) * 2 + core


def parts(gx, gy):
    return lax.div(gx, 4), lax.rem(gx, 4), lax.div(gy, 8), lax.rem(lax.div(gy, 2), 4), lax.rem(gy, 2)


def tile_of(gx, gy):
    hi_x, z, lo_x, y, core = parts(gx, gy)
    lo_x = lax.rem(lo_x + hi_x, 2)
    z = jnp.where(hi_x == 0, 3 - z, z)
    y = jnp.where(lo_x == 1, 3 - y, y)
    return place(hi_x, lo_x, y, z, core)


def device_of(gx, gy):
    hi_x, z, lo_x, y, core = parts(gx, gy)
    z = jnp.where(hi_x == 0, 3 - z, z)
    y = jnp.where(lo_x == 1, 3 - y, y)
    return place(hi_x, lax.rem(lo_x + hi_x, 2), y, z, core)


def cmul(ar, ai, br, bi):
    return ar * br - ai * bi, ar * bi + ai * br


def kernel(
    offs_in, cnt_in, obj, probe_in, prop_in, inten_in, w_in, out,
    o0, o1, d, z, r, a, q, psi, pat, tile, inten, fin, goal, probe, prop, w, offs, cnt,
    ssem, rsem, in_send, in_recv, out_send, out_recv, lsem,
):
    objects = (o0, o1)
    me = (lax.axis_index("gx"), lax.axis_index("gy"))
    gx, gy = tile_of(*me)
    core = lax.rem(gy, 2)
    home = (gx, gy)
    worker = device_of(*me)
    moved = jnp.logical_or(gx != me[0], gy != me[1])
    stays = jnp.logical_not(moved)
    has_u = gx > 0
    has_d = gx < 7
    has_o = jnp.logical_and(gy > 0, gy < 15)
    up = device_of(jnp.maximum(gx - 1, 0), gy)
    dn = device_of(jnp.minimum(gx + 1, 7), gy)
    mate = device_of(gx, gy + 1 - 2 * core)
    outer = device_of(gx, jnp.clip(gy - 1 + 2 * core, 0, 15))
    hl = 1 - core
    hr = core

    lane = lax.broadcasted_iota(jnp.int32, (1, N), 1)
    row = lax.broadcasted_iota(jnp.int32, (2 * N, N), 0)
    row_ok = jnp.logical_and(row >= jnp.where(gx == 0, H, 0), row < jnp.where(gx == 7, 3 * H, 4 * H))
    l_ok = lane >= jnp.where(gy == 0, H, 0)
    r_ok = lane < jnp.where(gy == 15, H, N)

    def desc(kind, src, dst, s, slot, dev):
        return pltpu.make_async_remote_copy(
            src_ref=src,
            dst_ref=dst,
            send_sem=ssem.at[kind, s, slot],
            recv_sem=rsem.at[kind, s, slot],
            device_id=dev,
            device_id_type=MESH,
        )

    def up_rows(mode):
        return {FIRST: (pl.ds(H, H), pl.ds(3 * H, H)), USUAL: (TOP, BOT), LAST: (pl.ds(0, H), pl.ds(N, H))}[mode]

    def down_rows(mode):
        return {FIRST: (pl.ds(N, H), pl.ds(0, H)), USUAL: (BOT, TOP), LAST: (pl.ds(3 * H, H), pl.ds(H, H))}[mode]

    def first_rows(mode):
        return pl.ds(H, N) if mode == FIRST else ALL

    def last_rows(mode):
        return pl.ds(H, N) if mode == LAST else ALL

    def along_z(kind, src, group, s, slot, mode, upward):
        (rows, landing), dev = (up_rows(mode), up) if upward else (down_rows(mode), dn)
        return desc(kind, src.at[rows], r.at[group, s, slot, landing], s, slot, dev)

    def copy(kind, s, slot, mode):
        if kind == K_YRE:
            rows = first_rows(mode)
            return desc(kind, d.at[s, 1, 0, rows], r.at[Y_RE, s, slot, rows], s, slot, outer)
        if kind in (K_ZIM_U, K_ZIM_D):
            return along_z(kind, d.at[s, 1, 1], Z_IM, s, slot, FIRST if mode == FIRST else USUAL, kind == K_ZIM_U)
        if kind == K_M:
            rows = first_rows(mode)
            return desc(kind, d.at[s, 0, 1 - core, rows], r.at[M_RS, s, slot, rows], s, slot, mate)
        if kind in (K_ZM_U, K_ZM_D):
            early = s == 1 and mode == LAST
            return along_z(kind, a.at[2, s], Z_M, s, slot, USUAL if early else mode, kind == K_ZM_U)
        if kind in (K_ZRE_U, K_ZRE_D):
            return along_z(kind, a.at[0, s], Z_RE, s, slot, mode, kind == K_ZRE_U)
        rows = last_rows(mode)
        if kind == K_YIM:
            return desc(kind, a.at[1, s, rows], r.at[Y_IM, s, slot, rows], s, slot, outer)
        return desc(kind, objects[s].at[0, core, rows], objects[s].at[0, core, rows], s, slot, mate)

    def landed(kind, s, slot, mode):
        if kind == K_P3:
            rows = last_rows(mode)
            return desc(kind, objects[s].at[0, core, rows], objects[s].at[0, 1 - core, rows], s, slot, mate)
        return copy(kind, s, slot, mode)

    has_no = jnp.logical_not(has_o)
    senders = {
        K_YRE: has_o, K_ZIM_U: has_u, K_ZIM_D: has_d, K_M: None, K_ZM_U: has_u, K_ZM_D: has_d,
        K_ZRE_U: has_u, K_ZRE_D: has_d, K_YIM: has_o, K_P3: None,
    }
    other_way = {K_ZIM_U: K_ZIM_D, K_ZM_U: K_ZM_D, K_ZRE_U: K_ZRE_D}
    other_way.update({v: k for k, v in other_way.items()})

    def guarded(cond, fn):
        if cond is None:
            fn()
        else:
            pl.when(cond)(fn)

    def send(kind, s, slot, mode):
        guarded(senders[kind], lambda: copy(kind, s, slot, mode).start())

    def recv(kind, s, slot, mode):
        guarded(senders[other_way.get(kind, kind)], lambda: landed(kind, s, slot, mode).wait_recv())

    def sent(kind, s, slot, mode):
        guarded(senders[kind], lambda: copy(kind, s, slot, mode).wait_send())

    def start(s, slot, mode):
        send(K_M, s, slot, mode)
        send(K_YRE, s, slot, mode)
        send(K_ZIM_U, s, slot, mode)
        send(K_ZIM_D, s, slot, mode)

    def mid_m(s, slot, mode):
        recv(K_M, s, slot, mode)
        a[2, s] = d[s, 0, core] + r[M_RS, s, slot]
        send(K_ZM_U, s, slot, mode)
        send(K_ZM_D, s, slot, mode)

    def mid_re(s, slot, mode):
        recv(K_YRE, s, slot, mode)
        a[0, s] = d[s, 1, 0] + r[Y_RE, s, slot]
        send(K_ZRE_U, s, slot, mode)
        send(K_ZRE_D, s, slot, mode)

    def mid_im(s, slot, mode):
        recv(K_ZIM_U, s, slot, mode)
        recv(K_ZIM_D, s, slot, mode)
        a[1, s] = d[s, 1, 1] + r[Z_IM, s, slot]
        send(K_YIM, s, slot, mode)

    def mid_back(s, slot, mode):
        recv(K_ZM_U, s, slot, mode)
        recv(K_ZM_D, s, slot, mode)
        objects[s][0, core] = objects[s][0, core] + (a[2, s] + r[Z_M, s, slot])
        send(K_P3, s, slot, mode)

    def finish(s, slot, mode):
        recv(K_ZRE_U, s, slot, mode)
        recv(K_ZRE_D, s, slot, mode)
        objects[s][1, 0] = objects[s][1, 0] + (a[0, s] + r[Z_RE, s, slot])
        recv(K_YIM, s, slot, mode)
        objects[s][1, 1] = objects[s][1, 1] + (a[1, s] + r[Y_IM, s, slot])
        recv(K_P3, s, slot, mode)
        for kind in range(10):
            sent(kind, s, slot, mode)

    def exchange(slot, mode):
        mid_m(0, slot, mode)
        mid_m(1, slot, USUAL)
        mid_im(1, slot, mode)
        mid_re(0, slot, mode)
        mid_im(0, slot, mode)
        mid_re(1, slot, mode)
        mid_back(0, slot, mode)
        mid_back(1, slot, mode)
        if mode == LAST:
            finish(1, slot, mode)
            give(1)
        finish(0, slot, mode)

    def send_home(s):
        return pltpu.make_async_remote_copy(
            src_ref=fin.at[s],
            dst_ref=out.at[s],
            send_sem=out_send.at[s],
            recv_sem=out_recv.at[s],
            device_id=home,
            device_id_type=MESH,
        )

    def give(s):
        for c in range(2):
            left = objects[s][hl, c, pl.ds(H, N), :]
            right = objects[s][hr, c, pl.ds(H, N), :]
            fin[s, c] = pltpu.roll(jnp.where(lane >= H, left, right), H, 1)
        pl.when(moved)(lambda: send_home(s).start())

        @pl.when(stays)
        def _():
            out[s] = fin[s]

    inputs = [(offs_in, offs), (cnt_in, cnt)]
    inputs += [(obj.at[s], tile.at[s]) for s in range(2)]

    def pass_on(i, src, dst):
        return pltpu.make_async_remote_copy(
            src_ref=src,
            dst_ref=dst,
            send_sem=in_send.at[i],
            recv_sem=in_recv.at[i],
            device_id=worker,
            device_id_type=MESH,
        )

    def keep(i, src, dst):
        return pltpu.make_async_copy(src, dst, in_send.at[i])

    def pass_start(i, src, dst):
        pl.when(moved)(lambda: pass_on(i, src, dst).start())
        pl.when(stays)(lambda: keep(i, src, dst).start())

    def pass_wait(i, src, dst):
        @pl.when(moved)
        def _():
            pass_on(i, src, dst).wait_send()
            pass_on(i, src, dst).wait_recv()

        pl.when(stays)(lambda: keep(i, src, dst).wait())

    def frames(b):
        return 4 + b, inten_in.at[pl.ds(BATCH * b, BATCH)], inten.at[pl.ds(BATCH * b, BATCH)]

    consts = [(probe_in, probe), (prop_in, prop), (w_in, w)]
    barrier = pltpu.get_barrier_semaphore()
    greet = ((None, mate), (has_u, up), (has_d, dn), (has_o, outer), (moved, home), (moved, worker))
    for cond, dev in greet:
        guarded(cond, lambda dev=dev: pl.semaphore_signal(barrier, inc=1, device_id=dev, device_id_type=MESH))
    for i, (src, dst) in enumerate(consts):
        pltpu.make_async_copy(src, dst, lsem.at[i]).start()
    count = 1 + sum(jnp.where(cond, 1, 0) for cond, _ in greet[1:])
    pl.semaphore_wait(barrier, count)
    for i in (2, 0, 1):
        pass_start(i, *inputs[i])
    for o in objects:
        o[...] = jnp.zeros_like(o)
    d[...] = jnp.zeros_like(d)
    z[...] = jnp.zeros_like(z)
    for group, rows in ((Y_RE, ((0, H), (3 * H, H))), (M_RS, ((0, H), (3 * H, H)))):
        for first, n in rows:
            r[group, :, 0, pl.ds(first, n)] = jnp.zeros((2, n, N), F32)
    for group in (Z_IM, Z_M, Z_RE):
        r[group, :, 0, pl.ds(H, N)] = jnp.zeros((2, N, N), F32)

    @pl.when(gx == 0)
    def _():
        for group in (Z_IM, Z_M, Z_RE):
            r[group, :, :, TOP] = jnp.zeros((2, 2, N, N), F32)

    @pl.when(gx == 7)
    def _():
        for group in (Z_IM, Z_M, Z_RE):
            r[group, :, :, BOT] = jnp.zeros((2, 2, N, N), F32)

    @pl.when(has_no)
    def _():
        for group in (Y_RE, Y_IM):
            r[group] = jnp.zeros((2, 2, 2 * N, N), F32)

    for i, (src, dst) in enumerate(consts):
        pltpu.make_async_copy(src, dst, lsem.at[i]).wait()
    q[0] = jnp.cos(prop[...]).T
    q[1] = jnp.sin(prop[...]).T
    pass_start(3, *inputs[3])

    def begin(s):
        pass_wait(2 + s, *inputs[2 + s])
        for c in range(2):
            cells = pltpu.roll(tile[s, c], H, 1)
            d[s, hl, c, pl.ds(H, N)] = jnp.where(lane >= H, cells, 0.0)
            d[s, hr, c, pl.ds(H, N)] = jnp.where(lane < H, cells, 0.0)
        start(s, 0, FIRST)

    begin(0)
    mid_m(0, 0, FIRST)
    begin(1)
    pass_start(*frames(0))
    mid_re(0, 0, FIRST)
    mid_im(0, 0, FIRST)
    mid_m(1, 0, FIRST)
    mid_back(0, 0, FIRST)
    mid_re(1, 0, FIRST)
    mid_im(1, 0, FIRST)
    mid_back(1, 0, FIRST)
    for i in range(2):
        pass_wait(i, *inputs[i])
    finish(0, 0, FIRST)

    def split(x):
        hi = x.astype(BF16)
        return hi, (x - hi.astype(F32)).astype(BF16)

    def transform(re, im, inverse):
        right = jnp.concatenate([w[inverse, 0], w[inverse, 0], w[inverse, 1]], 0)

        def product(x, y):
            hi, lo = split(jnp.concatenate([x, y], 1))
            z = jnp.dot(jnp.concatenate([hi, lo, hi], 1), right, preferred_element_type=F32)
            return z[:, :N], z[:, N:]

        first = [product(re[m], im[m]) for m in range(BATCH)]
        second = [product(x.T, y.T) for x, y in first]
        return [x for x, _ in second], [y for _, y in second]

    def patch(s, c, r0, q0):
        left = objects[s][hl, c, pl.ds(r0, N), :]
        right = objects[s][hr, c, pl.ds(r0, N), :]
        return pltpu.roll(jnp.where(lane >= q0, left, right), (N - q0) & (N - 1), 1)

    def scatter(s, places, grads):
        for m in range(BATCH):
            r0, q0, weight = places[m]
            fl = jnp.where(jnp.logical_and(lane >= q0, l_ok), weight, 0.0)
            fr = jnp.where(jnp.logical_and(lane < q0, r_ok), weight, 0.0)
            for c in range(2):
                g = pltpu.roll(grads[c][m], q0 & (N - 1), 1)
                z[m, 0, c, pl.ds(N, N)] = g * fl
                z[m, 1, c, pl.ds(N, N)] = g * fr
        for h, half in ((0, hl), (1, hr)):
            for c in range(2):
                total = z[0, h, c, pl.ds(N - places[0][0], 2 * N), :] + z[1, h, c, pl.ds(N - places[1][0], 2 * N), :]
                d[s, half, c] = jnp.where(row_ok, total, 0.0)

    def batch(b, carry):
        slot = lax.rem(b + 1, 2)
        before = lax.rem(b, 2)
        pl.when(b < NB - 1)(lambda: pass_start(*frames(b + 1)))
        places = []
        for m in range(BATCH):
            n = b * BATCH + m
            weight = jnp.where(n < cnt[0, 0], -STEP, 0.0).astype(F32)
            places.append((offs[0, n], offs[1, n], weight))
        pr, pi = probe[0], probe[1]
        re, im = [], []
        for m in range(BATCH):
            r0, q0, _ = places[m]
            x, y = cmul(pr, pi, patch(0, 0, r0, q0), patch(0, 1, r0, q0))
            re.append(x)
            im.append(y)
        re, im = transform(re, im, 0)
        both = [cmul(re[m], im[m], q[0], q[1]) for m in range(BATCH)]
        re, im = transform([x for x, _ in both], [y for _, y in both], 1)
        for m in range(BATCH):
            psi[m, 0] = re[m]
            psi[m, 1] = im[m]
        pass_wait(*frames(b))
        for m in range(BATCH):
            goal[m] = inten[b * BATCH + m].T
        pl.when(b == 0)(lambda: finish(1, before, FIRST))
        pl.when(b > 0)(lambda: finish(1, before, USUAL))
        both = []
        for m in range(BATCH):
            r0, q0, _ = places[m]
            for c in range(2):
                pat[m, c] = patch(1, c, r0, q0)
            both.append(cmul(psi[m, 0], psi[m, 1], pat[m, 0], pat[m, 1]))
        re, im = transform([x for x, _ in both], [y for _, y in both], 0)
        excess = [re[m] * re[m] + im[m] * im[m] - goal[m] for m in range(BATCH)]
        re, im = transform([excess[m] * re[m] for m in range(BATCH)], [excess[m] * im[m] for m in range(BATCH)], 1)
        both = [cmul(psi[m, 0], -psi[m, 1], re[m], im[m]) for m in range(BATCH)]
        scatter(1, places, ([x for x, _ in both], [y for _, y in both]))
        start(1, slot, USUAL)
        both = [cmul(pat[m, 0], -pat[m, 1], re[m], im[m]) for m in range(BATCH)]
        re, im = transform([x for x, _ in both], [y for _, y in both], 0)
        both = [cmul(re[m], im[m], q[0], -q[1]) for m in range(BATCH)]
        re, im = transform([x for x, _ in both], [y for _, y in both], 1)
        both = [cmul(re[m], im[m], pr, -pi) for m in range(BATCH)]
        scatter(0, places, ([x for x, _ in both], [y for _, y in both]))
        start(0, slot, USUAL)
        pl.when(b < NB - 1)(lambda: exchange(slot, USUAL))
        pl.when(b == NB - 1)(lambda: exchange(slot, LAST))
        return carry

    lax.fori_loop(0, NB, batch, 0)
    give(0)
    for s in range(2):
        @pl.when(moved)
        def _():
            send_home(s).wait_send()
            send_home(s).wait_recv()


def solution(mesh):
    tables = dft_tables()

    def local(object_field, probe, propagator, offsets, counts, intensity):
        hbm = pl.BlockSpec(memory_space=pltpu.HBM)
        return pl.pallas_call(
            kernel,
            out_shape=jax.ShapeDtypeStruct((2, 2, N, N), F32),
            in_specs=[hbm] * 7,
            out_specs=pl.BlockSpec(memory_space=pltpu.VMEM),
            scratch_shapes=[
                pltpu.VMEM((2, 2, 2 * N, N), F32),
                pltpu.VMEM((2, 2, 2 * N, N), F32),
                pltpu.VMEM((2, 2, 2, 2 * N, N), F32),
                pltpu.VMEM((BATCH, 2, 2, 3 * N, N), F32),
                pltpu.VMEM((6, 2, 2, 2 * N, N), F32),
                pltpu.VMEM((3, 2, 2 * N, N), F32),
                pltpu.VMEM((2, N, N), F32),
                pltpu.VMEM((BATCH, 2, N, N), F32),
                pltpu.VMEM((BATCH, 2, N, N), F32),
                pltpu.VMEM((2, 2, N, N), F32),
                pltpu.VMEM((NB * BATCH, N, N), F32),
                pltpu.VMEM((2, 2, N, N), F32),
                pltpu.VMEM((BATCH, N, N), F32),
                pltpu.VMEM((2, N, N), F32),
                pltpu.VMEM((N, N), F32),
                pltpu.VMEM((2, 2, 2 * N, 2 * N), BF16),
                pltpu.SMEM((2, NB * BATCH), jnp.int32),
                pltpu.SMEM((1, 1), jnp.int32),
                pltpu.SemaphoreType.DMA((10, 2, 2)),
                pltpu.SemaphoreType.DMA((10, 2, 2)),
                pltpu.SemaphoreType.DMA((4 + NB,)),
                pltpu.SemaphoreType.DMA((4 + NB,)),
                pltpu.SemaphoreType.DMA((2,)),
                pltpu.SemaphoreType.DMA((2,)),
                pltpu.SemaphoreType.DMA((3,)),
            ],
            compiler_params=pltpu.CompilerParams(
                collective_id=0, has_side_effects=True, vmem_limit_bytes=58 * 1024 * 1024
            ),
        )(
            offsets[0, 0].T, counts, object_field, probe, propagator, intensity[0, 0], jnp.asarray(tables),
        )

    in_specs = (
        P(None, None, "gx", "gy"),
        P(),
        P(),
        P("gx", "gy", None, None),
        P("gx", "gy"),
        P("gx", "gy", None, None, None),
    )
    out_specs = P(None, None, "gx", "gy")
    return jax.shard_map(local, mesh=mesh, in_specs=in_specs, out_specs=out_specs, check_vma=False)
```

```python
import math

import jax
import jax.numpy as jnp
import ml_dtypes
import numpy as np
from jax import lax
from jax.experimental import pallas as pl
from jax.experimental.pallas import tpu as pltpu
from jax.sharding import PartitionSpec as P

MESH = pl.DeviceIdType.MESH
N = 128
H = 64
BATCH = 2
NB = 6
STEP = 0.08
F32 = jnp.float32
BF16 = jnp.bfloat16

Y_RE, Z_IM, M_RS, Z_M, Z_RE, Y_IM = range(6)
K_YRE, K_ZIM_U, K_ZIM_D, K_M, K_ZM_U, K_ZM_D, K_ZRE_U, K_ZRE_D, K_YIM, K_P3 = range(10)
K_YRE_T, K_YRE_B, K_ZIM_U2, K_ZIM_D2, K_ZRE_U2, K_ZRE_D2, K_YIM_T, K_YIM_B = range(10, 18)
KINDS = 18
FIRST, USUAL, LAST = range(3)
ALL = pl.ds(0, 2 * N)
TOP = pl.ds(0, N)
BOT = pl.ds(N, N)


def dft_tables():
    index = np.arange(N)
    phase = (index[:, None] * index[None, :] % N) * (2.0 * math.pi / N)
    c, s = np.cos(phase) / math.sqrt(N), np.sin(phase) / math.sqrt(N)
    out = []
    for sign in (-1.0, 1.0):
        m = np.block([[c, sign * s], [-sign * s, c]])
        hi = m.astype(ml_dtypes.bfloat16)
        out.append(np.stack([hi, (m - hi.astype(np.float64)).astype(ml_dtypes.bfloat16)]))
    return np.stack(out)


def place(hi_x, lo_x, y, z, core):
    return hi_x * 4 + z, (lo_x * 4 + y) * 2 + core


def parts(gx, gy):
    return lax.div(gx, 4), lax.rem(gx, 4), lax.div(gy, 8), lax.rem(lax.div(gy, 2), 4), lax.rem(gy, 2)


def tile_of(gx, gy):
    hi_x, z, lo_x, y, core = parts(gx, gy)
    lo_x = lax.rem(lo_x + hi_x, 2)
    z = jnp.where(hi_x == 0, 3 - z, z)
    y = jnp.where(lo_x == 1, 3 - y, y)
    return place(hi_x, lo_x, y, z, core)


def device_of(gx, gy):
    hi_x, z, lo_x, y, core = parts(gx, gy)
    z = jnp.where(hi_x == 0, 3 - z, z)
    y = jnp.where(lo_x == 1, 3 - y, y)
    return place(hi_x, lax.rem(lo_x + hi_x, 2), y, z, core)


def cmul(ar, ai, br, bi):
    return ar * br - ai * bi, ar * bi + ai * br


def kernel(
    offs_in, cnt_in, obj, probe_in, prop_in, inten_in, w_in, out,
    o0, o1, d, z, r, a, q, psi, pat, tile, inten, fin, goal, probe, prop, w, offs, cnt,
    ssem, rsem, in_send, in_recv, out_send, out_recv, lsem,
):
    objects = (o0, o1)
    me = (lax.axis_index("gx"), lax.axis_index("gy"))
    gx, gy = tile_of(*me)
    core = lax.rem(gy, 2)
    home = (gx, gy)
    worker = device_of(*me)
    moved = jnp.logical_or(gx != me[0], gy != me[1])
    stays = jnp.logical_not(moved)
    has_u = gx > 0
    has_d = gx < 7
    has_o = jnp.logical_and(gy > 0, gy < 15)
    up = device_of(jnp.maximum(gx - 1, 0), gy)
    dn = device_of(jnp.minimum(gx + 1, 7), gy)
    mate = device_of(gx, gy + 1 - 2 * core)
    outer = device_of(gx, jnp.clip(gy - 1 + 2 * core, 0, 15))
    hl = 1 - core
    hr = core

    lane = lax.broadcasted_iota(jnp.int32, (1, N), 1)
    row = lax.broadcasted_iota(jnp.int32, (2 * N, N), 0)
    row_ok = jnp.logical_and(row >= jnp.where(gx == 0, H, 0), row < jnp.where(gx == 7, 3 * H, 4 * H))
    l_ok = lane >= jnp.where(gy == 0, H, 0)
    r_ok = lane < jnp.where(gy == 15, H, N)

    def desc(kind, src, dst, s, slot, dev):
        return pltpu.make_async_remote_copy(
            src_ref=src,
            dst_ref=dst,
            send_sem=ssem.at[kind, s, slot],
            recv_sem=rsem.at[kind, s, slot],
            device_id=dev,
            device_id_type=MESH,
        )

    def up_rows(mode):
        return {FIRST: (pl.ds(H, H), pl.ds(3 * H, H)), USUAL: (TOP, BOT), LAST: (pl.ds(0, H), pl.ds(N, H))}[mode]

    def down_rows(mode):
        return {FIRST: (pl.ds(N, H), pl.ds(0, H)), USUAL: (BOT, TOP), LAST: (pl.ds(3 * H, H), pl.ds(H, H))}[mode]

    def first_rows(mode):
        return pl.ds(H, N) if mode == FIRST else ALL

    def last_rows(mode):
        return pl.ds(H, N) if mode == LAST else ALL

    def live(kind, s, mode):
        if s == 1:
            return kind < 10
        if kind in (K_YRE_T, K_YRE_B, K_ZIM_U2, K_ZIM_D2, K_ZRE_U2, K_ZRE_D2):
            return mode != FIRST
        if kind in (K_ZRE_U, K_ZRE_D, K_YIM_T, K_YIM_B):
            return mode != LAST
        return True

    def along_z(kind, src, group, s, slot, mode, upward):
        (rows, landing), dev = (up_rows(mode), up) if upward else (down_rows(mode), dn)
        return desc(kind, src.at[rows], r.at[group, s, slot, landing], s, slot, dev)

    def copy(kind, s, slot, mode):
        if kind in (K_YRE, K_YRE_T, K_YRE_B):
            rows = first_rows(FIRST if s == 0 else mode)
            rows = {K_YRE_T: pl.ds(0, H), K_YRE_B: pl.ds(3 * H, H)}.get(kind, rows)
            return desc(kind, d.at[s, 1, 0, rows], r.at[Y_RE, s, slot, rows], s, slot, outer)
        if kind in (K_ZIM_U2, K_ZIM_D2):
            return along_z(kind, d.at[s, 1, 1], Z_IM, s, slot, LAST, kind == K_ZIM_U2)
        if kind in (K_ZRE_U2, K_ZRE_D2):
            return along_z(kind, a.at[0, s], Z_RE, s, slot, LAST, kind == K_ZRE_U2)
        if kind in (K_ZIM_U, K_ZIM_D):
            piece = FIRST if s == 0 or mode == FIRST else USUAL
            return along_z(kind, d.at[s, 1, 1], Z_IM, s, slot, piece, kind == K_ZIM_U)
        if kind == K_M:
            rows = first_rows(mode)
            return desc(kind, d.at[s, 0, 1 - core, rows], r.at[M_RS, s, slot, rows], s, slot, mate)
        if kind in (K_ZM_U, K_ZM_D):
            early = s == 1 and mode == LAST
            return along_z(kind, a.at[2, s], Z_M, s, slot, USUAL if early else mode, kind == K_ZM_U)
        if kind in (K_ZRE_U, K_ZRE_D):
            return along_z(kind, a.at[0, s], Z_RE, s, slot, FIRST if s == 0 else mode, kind == K_ZRE_U)
        rows = last_rows(mode)
        if kind in (K_YIM, K_YIM_T, K_YIM_B):
            rows = pl.ds(H, N) if s == 0 else rows
            rows = {K_YIM_T: pl.ds(0, H), K_YIM_B: pl.ds(3 * H, H)}.get(kind, rows)
            return desc(kind, a.at[1, s, rows], r.at[Y_IM, s, slot, rows], s, slot, outer)
        return desc(kind, objects[s].at[0, core, rows], objects[s].at[0, core, rows], s, slot, mate)

    def landed(kind, s, slot, mode):
        if kind == K_P3:
            rows = last_rows(mode)
            return desc(kind, objects[s].at[0, core, rows], objects[s].at[0, 1 - core, rows], s, slot, mate)
        return copy(kind, s, slot, mode)

    has_no = jnp.logical_not(has_o)
    senders = {
        K_YRE: has_o, K_ZIM_U: has_u, K_ZIM_D: has_d, K_M: None, K_ZM_U: has_u, K_ZM_D: has_d,
        K_ZRE_U: has_u, K_ZRE_D: has_d, K_YIM: has_o, K_P3: None,
        K_YRE_T: has_o, K_YRE_B: has_o, K_ZIM_U2: has_u, K_ZIM_D2: has_d,
        K_ZRE_U2: has_u, K_ZRE_D2: has_d, K_YIM_T: has_o, K_YIM_B: has_o,
    }
    other_way = {K_ZIM_U: K_ZIM_D, K_ZM_U: K_ZM_D, K_ZRE_U: K_ZRE_D, K_ZIM_U2: K_ZIM_D2, K_ZRE_U2: K_ZRE_D2}
    other_way.update({v: k for k, v in other_way.items()})

    def guarded(cond, fn):
        if cond is None:
            fn()
        else:
            pl.when(cond)(fn)

    def send(kind, s, slot, mode):
        if live(kind, s, mode):
            guarded(senders[kind], lambda: copy(kind, s, slot, mode).start())

    def recv(kind, s, slot, mode):
        if live(kind, s, mode):
            guarded(senders[other_way.get(kind, kind)], lambda: landed(kind, s, slot, mode).wait_recv())

    def sent(kind, s, slot, mode):
        if live(kind, s, mode):
            guarded(senders[kind], lambda: copy(kind, s, slot, mode).wait_send())

    def start(s, slot, mode):
        send(K_M, s, slot, mode)
        send(K_YRE, s, slot, mode)
        send(K_ZIM_U, s, slot, mode)
        send(K_ZIM_D, s, slot, mode)

    def mid_m(s, slot, mode):
        recv(K_M, s, slot, mode)
        a[2, s] = d[s, 0, core] + r[M_RS, s, slot]
        send(K_ZM_U, s, slot, mode)
        send(K_ZM_D, s, slot, mode)

    def mid_re(s, slot, mode):
        recv(K_YRE, s, slot, mode)
        a[0, s] = d[s, 1, 0] + r[Y_RE, s, slot]
        send(K_ZRE_U, s, slot, mode)
        send(K_ZRE_D, s, slot, mode)

    def mid_im(s, slot, mode):
        recv(K_ZIM_U, s, slot, mode)
        recv(K_ZIM_D, s, slot, mode)
        a[1, s] = d[s, 1, 1] + r[Z_IM, s, slot]
        send(K_YIM, s, slot, mode)

    def rims_and_middle(mode):
        rims, middle = [pl.ds(0, H), pl.ds(3 * H, H)], [pl.ds(H, N)]
        return (rims, middle) if mode != FIRST else ([], [ALL])

    def re_first(slot, mode):
        recv(K_YRE, 0, slot, mode)
        for rows in rims_and_middle(mode)[1]:
            a[0, 0, rows] = d[0, 1, 0, rows] + r[Y_RE, 0, slot, rows]
        send(K_ZRE_U, 0, slot, mode)
        send(K_ZRE_D, 0, slot, mode)

    def re_second(slot, mode):
        recv(K_YRE_T, 0, slot, mode)
        recv(K_YRE_B, 0, slot, mode)
        for rows in rims_and_middle(mode)[0]:
            a[0, 0, rows] = d[0, 1, 0, rows] + r[Y_RE, 0, slot, rows]
        send(K_ZRE_U2, 0, slot, mode)
        send(K_ZRE_D2, 0, slot, mode)

    def im_first(slot, mode):
        recv(K_ZIM_U2, 0, slot, mode)
        recv(K_ZIM_D2, 0, slot, mode)
        if mode != FIRST:
            a[1, 0, pl.ds(H, N)] = d[0, 1, 1, pl.ds(H, N)] + r[Z_IM, 0, slot, pl.ds(H, N)]
            send(K_YIM, 0, slot, mode)

    def im_second(slot, mode):
        recv(K_ZIM_U, 0, slot, mode)
        recv(K_ZIM_D, 0, slot, mode)
        for rows in [ALL] if mode == FIRST else rims_and_middle(mode)[0]:
            a[1, 0, rows] = d[0, 1, 1, rows] + r[Z_IM, 0, slot, rows]
        send(K_YIM_T, 0, slot, mode)
        send(K_YIM_B, 0, slot, mode)
        if mode == FIRST:
            send(K_YIM, 0, slot, mode)

    def mid_back(s, slot, mode):
        recv(K_ZM_U, s, slot, mode)
        recv(K_ZM_D, s, slot, mode)
        objects[s][0, core] = objects[s][0, core] + (a[2, s] + r[Z_M, s, slot])
        send(K_P3, s, slot, mode)

    def finish(s, slot, mode):
        for kind in (K_ZRE_U, K_ZRE_D, K_ZRE_U2, K_ZRE_D2):
            recv(kind, s, slot, mode)
        objects[s][1, 0] = objects[s][1, 0] + (a[0, s] + r[Z_RE, s, slot])
        for kind in (K_YIM, K_YIM_T, K_YIM_B):
            recv(kind, s, slot, mode)
        objects[s][1, 1] = objects[s][1, 1] + (a[1, s] + r[Y_IM, s, slot])
        recv(K_P3, s, slot, mode)

    def all_sent(slot, mode):
        for s in range(2):
            for kind in range(KINDS):
                sent(kind, s, slot, mode)

    def exchange(slot, mode):
        mid_m(0, slot, mode)
        mid_m(1, slot, USUAL)
        mid_im(1, slot, mode)
        re_first(slot, mode)
        im_first(slot, mode)
        re_second(slot, mode)
        im_second(slot, mode)
        mid_re(1, slot, mode)
        mid_back(0, slot, mode)
        mid_back(1, slot, mode)
        if mode == LAST:
            finish(1, slot, mode)
            give(1)
        all_sent(slot, mode)
        finish(0, slot, mode)

    def send_home(s):
        return pltpu.make_async_remote_copy(
            src_ref=fin.at[s],
            dst_ref=out.at[s],
            send_sem=out_send.at[s],
            recv_sem=out_recv.at[s],
            device_id=home,
            device_id_type=MESH,
        )

    def give(s):
        for c in range(2):
            left = objects[s][hl, c, pl.ds(H, N), :]
            right = objects[s][hr, c, pl.ds(H, N), :]
            fin[s, c] = pltpu.roll(jnp.where(lane >= H, left, right), H, 1)
        pl.when(moved)(lambda: send_home(s).start())

        @pl.when(stays)
        def _():
            out[s] = fin[s]

    inputs = [(offs_in, offs), (cnt_in, cnt)]
    inputs += [(obj.at[s], tile.at[s]) for s in range(2)]

    def pass_on(i, src, dst):
        return pltpu.make_async_remote_copy(
            src_ref=src,
            dst_ref=dst,
            send_sem=in_send.at[i],
            recv_sem=in_recv.at[i],
            device_id=worker,
            device_id_type=MESH,
        )

    def keep(i, src, dst):
        return pltpu.make_async_copy(src, dst, in_send.at[i])

    def pass_start(i, src, dst):
        pl.when(moved)(lambda: pass_on(i, src, dst).start())
        pl.when(stays)(lambda: keep(i, src, dst).start())

    def pass_wait(i, src, dst):
        @pl.when(moved)
        def _():
            pass_on(i, src, dst).wait_send()
            pass_on(i, src, dst).wait_recv()

        pl.when(stays)(lambda: keep(i, src, dst).wait())

    def frames(b):
        return 4 + b, inten_in.at[pl.ds(BATCH * b, BATCH)], inten.at[pl.ds(BATCH * b, BATCH)]

    consts = [(probe_in, probe), (prop_in, prop), (w_in, w)]
    barrier = pltpu.get_barrier_semaphore()
    greet = ((None, mate), (has_u, up), (has_d, dn), (has_o, outer), (moved, home), (moved, worker))
    for cond, dev in greet:
        guarded(cond, lambda dev=dev: pl.semaphore_signal(barrier, inc=1, device_id=dev, device_id_type=MESH))
    for i, (src, dst) in enumerate(consts):
        pltpu.make_async_copy(src, dst, lsem.at[i]).start()
    count = 1 + sum(jnp.where(cond, 1, 0) for cond, _ in greet[1:])
    pl.semaphore_wait(barrier, count)
    for i in (2, 0, 1):
        pass_start(i, *inputs[i])
    for o in objects:
        o[...] = jnp.zeros_like(o)
    d[...] = jnp.zeros_like(d)
    z[...] = jnp.zeros_like(z)
    for group, rows in ((Y_RE, ((0, H), (3 * H, H))), (M_RS, ((0, H), (3 * H, H)))):
        for first, n in rows:
            r[group, :, 0, pl.ds(first, n)] = jnp.zeros((2, n, N), F32)
    for group in (Z_IM, Z_M, Z_RE):
        r[group, :, 0, pl.ds(H, N)] = jnp.zeros((2, N, N), F32)

    @pl.when(gx == 0)
    def _():
        for group in (Z_IM, Z_M, Z_RE):
            r[group, :, :, TOP] = jnp.zeros((2, 2, N, N), F32)

    @pl.when(gx == 7)
    def _():
        for group in (Z_IM, Z_M, Z_RE):
            r[group, :, :, BOT] = jnp.zeros((2, 2, N, N), F32)

    @pl.when(has_no)
    def _():
        for group in (Y_RE, Y_IM):
            r[group] = jnp.zeros((2, 2, 2 * N, N), F32)

    for i, (src, dst) in enumerate(consts):
        pltpu.make_async_copy(src, dst, lsem.at[i]).wait()
    q[0] = jnp.cos(prop[...]).T
    q[1] = jnp.sin(prop[...]).T
    pass_start(3, *inputs[3])

    def begin(s):
        pass_wait(2 + s, *inputs[2 + s])
        for c in range(2):
            cells = pltpu.roll(tile[s, c], H, 1)
            d[s, hl, c, pl.ds(H, N)] = jnp.where(lane >= H, cells, 0.0)
            d[s, hr, c, pl.ds(H, N)] = jnp.where(lane < H, cells, 0.0)
        start(s, 0, FIRST)

    begin(0)
    mid_m(0, 0, FIRST)
    begin(1)
    pass_start(*frames(0))
    re_first(0, FIRST)
    im_second(0, FIRST)
    mid_m(1, 0, FIRST)
    mid_back(0, 0, FIRST)
    mid_re(1, 0, FIRST)
    mid_im(1, 0, FIRST)
    mid_back(1, 0, FIRST)
    for i in range(2):
        pass_wait(i, *inputs[i])
    all_sent(0, FIRST)
    finish(0, 0, FIRST)

    def split(x):
        hi = x.astype(BF16)
        return hi, (x - hi.astype(F32)).astype(BF16)

    def transform(re, im, inverse):
        right = jnp.concatenate([w[inverse, 0], w[inverse, 0], w[inverse, 1]], 0)

        def product(x, y):
            hi, lo = split(jnp.concatenate([x, y], 1))
            z = jnp.dot(jnp.concatenate([hi, lo, hi], 1), right, preferred_element_type=F32)
            return z[:, :N], z[:, N:]

        first = [product(re[m], im[m]) for m in range(BATCH)]
        second = [product(x.T, y.T) for x, y in first]
        return [x for x, _ in second], [y for _, y in second]

    def patch(s, c, r0, q0):
        left = objects[s][hl, c, pl.ds(r0, N), :]
        right = objects[s][hr, c, pl.ds(r0, N), :]
        return pltpu.roll(jnp.where(lane >= q0, left, right), (N - q0) & (N - 1), 1)

    def scatter(s, slot, places, grads):
        for m in range(BATCH):
            r0, q0, weight = places[m]
            fl = jnp.where(jnp.logical_and(lane >= q0, l_ok), weight, 0.0)
            fr = jnp.where(jnp.logical_and(lane < q0, r_ok), weight, 0.0)
            for c in range(2):
                g = pltpu.roll(grads[c][m], q0 & (N - 1), 1)
                z[m, 0, c, pl.ds(N, N)] = g * fl
                z[m, 1, c, pl.ds(N, N)] = g * fr
        for half, side, planes in ((1, core, ((0, (K_YRE, K_YRE_T, K_YRE_B)), (1, (K_ZIM_U2, K_ZIM_D2, K_ZIM_U, K_ZIM_D)))), (0, 1 - core, ((1 - core, (K_M,)), (core, ())))):
            for c, kinds in planes:
                first = z[0, side, c, pl.ds(N - places[0][0], 2 * N), :]
                second = z[1, side, c, pl.ds(N - places[1][0], 2 * N), :]
                d[s, half, c] = jnp.where(row_ok, first + second, 0.0)
                for kind in kinds:
                    send(kind, s, slot, USUAL)

    def batch(b, carry):
        slot = lax.rem(b + 1, 2)
        before = lax.rem(b, 2)
        pl.when(b < NB - 1)(lambda: pass_start(*frames(b + 1)))
        places = []
        for m in range(BATCH):
            n = b * BATCH + m
            weight = jnp.where(n < cnt[0, 0], -STEP, 0.0).astype(F32)
            places.append((offs[0, n], offs[1, n], weight))
        pr, pi = probe[0], probe[1]
        re, im = [], []
        for m in range(BATCH):
            r0, q0, _ = places[m]
            x, y = cmul(pr, pi, patch(0, 0, r0, q0), patch(0, 1, r0, q0))
            re.append(x)
            im.append(y)
        re, im = transform(re, im, 0)
        both = [cmul(re[m], im[m], q[0], q[1]) for m in range(BATCH)]
        re, im = transform([x for x, _ in both], [y for _, y in both], 1)
        for m in range(BATCH):
            psi[m, 0] = re[m]
            psi[m, 1] = im[m]
        pass_wait(*frames(b))
        for m in range(BATCH):
            goal[m] = inten[b * BATCH + m].T
        pl.when(b == 0)(lambda: finish(1, before, FIRST))
        pl.when(b > 0)(lambda: finish(1, before, USUAL))
        both = []
        for m in range(BATCH):
            r0, q0, _ = places[m]
            for c in range(2):
                pat[m, c] = patch(1, c, r0, q0)
            both.append(cmul(psi[m, 0], psi[m, 1], pat[m, 0], pat[m, 1]))
        re, im = transform([x for x, _ in both], [y for _, y in both], 0)
        excess = [re[m] * re[m] + im[m] * im[m] - goal[m] for m in range(BATCH)]
        re, im = transform([excess[m] * re[m] for m in range(BATCH)], [excess[m] * im[m] for m in range(BATCH)], 1)
        both = [cmul(psi[m, 0], -psi[m, 1], re[m], im[m]) for m in range(BATCH)]
        scatter(1, slot, places, ([x for x, _ in both], [y for _, y in both]))
        both = [cmul(pat[m, 0], -pat[m, 1], re[m], im[m]) for m in range(BATCH)]
        re, im = transform([x for x, _ in both], [y for _, y in both], 0)
        both = [cmul(re[m], im[m], q[0], -q[1]) for m in range(BATCH)]
        re, im = transform([x for x, _ in both], [y for _, y in both], 1)
        both = [cmul(re[m], im[m], pr, -pi) for m in range(BATCH)]
        scatter(0, slot, places, ([x for x, _ in both], [y for _, y in both]))
        pl.when(b < NB - 1)(lambda: exchange(slot, USUAL))
        pl.when(b == NB - 1)(lambda: exchange(slot, LAST))
        return carry

    lax.fori_loop(0, NB, batch, 0)
    give(0)
    for s in range(2):
        @pl.when(moved)
        def _():
            send_home(s).wait_send()
            send_home(s).wait_recv()


def solution(mesh):
    tables = dft_tables()

    def local(object_field, probe, propagator, offsets, counts, intensity):
        hbm = pl.BlockSpec(memory_space=pltpu.HBM)
        return pl.pallas_call(
            kernel,
            out_shape=jax.ShapeDtypeStruct((2, 2, N, N), F32),
            in_specs=[hbm] * 7,
            out_specs=pl.BlockSpec(memory_space=pltpu.VMEM),
            scratch_shapes=[
                pltpu.VMEM((2, 2, 2 * N, N), F32),
                pltpu.VMEM((2, 2, 2 * N, N), F32),
                pltpu.VMEM((2, 2, 2, 2 * N, N), F32),
                pltpu.VMEM((BATCH, 2, 2, 3 * N, N), F32),
                pltpu.VMEM((6, 2, 2, 2 * N, N), F32),
                pltpu.VMEM((3, 2, 2 * N, N), F32),
                pltpu.VMEM((2, N, N), F32),
                pltpu.VMEM((BATCH, 2, N, N), F32),
                pltpu.VMEM((BATCH, 2, N, N), F32),
                pltpu.VMEM((2, 2, N, N), F32),
                pltpu.VMEM((NB * BATCH, N, N), F32),
                pltpu.VMEM((2, 2, N, N), F32),
                pltpu.VMEM((BATCH, N, N), F32),
                pltpu.VMEM((2, N, N), F32),
                pltpu.VMEM((N, N), F32),
                pltpu.VMEM((2, 2, 2 * N, 2 * N), BF16),
                pltpu.SMEM((2, NB * BATCH), jnp.int32),
                pltpu.SMEM((1, 1), jnp.int32),
                pltpu.SemaphoreType.DMA((KINDS, 2, 2)),
                pltpu.SemaphoreType.DMA((KINDS, 2, 2)),
                pltpu.SemaphoreType.DMA((4 + NB,)),
                pltpu.SemaphoreType.DMA((4 + NB,)),
                pltpu.SemaphoreType.DMA((2,)),
                pltpu.SemaphoreType.DMA((2,)),
                pltpu.SemaphoreType.DMA((3,)),
            ],
            compiler_params=pltpu.CompilerParams(
                collective_id=0, has_side_effects=True, vmem_limit_bytes=58 * 1024 * 1024
            ),
        )(
            offsets[0, 0].T, counts, object_field, probe, propagator, intensity[0, 0], jnp.asarray(tables),
        )

    in_specs = (
        P(None, None, "gx", "gy"),
        P(),
        P(),
        P("gx", "gy", None, None),
        P("gx", "gy"),
        P("gx", "gy", None, None, None),
    )
    out_specs = P(None, None, "gx", "gy")
    return jax.shard_map(local, mesh=mesh, in_specs=in_specs, out_specs=out_specs, check_vma=False)
```

```python
import math

import jax
import jax.numpy as jnp
import ml_dtypes
import numpy as np
from jax import lax
from jax.experimental import pallas as pl
from jax.experimental.pallas import tpu as pltpu
from jax.sharding import PartitionSpec as P

MESH = pl.DeviceIdType.MESH
N = 128
H = 64
BATCH = 2
NB = 6
STEP = 0.08
F32 = jnp.float32
BF16 = jnp.bfloat16

Y_RE, Z_IM, M_RS, Z_M, Z_RE, Y_IM = range(6)
K_YRE, K_ZIM_U, K_ZIM_D, K_M, K_ZM_U, K_ZM_D, K_ZRE_U, K_ZRE_D, K_YIM, K_P3 = range(10)
K_YRE_T, K_YRE_B, K_ZIM_U2, K_ZIM_D2, K_ZRE_U2, K_ZRE_D2, K_YIM_T, K_YIM_B = range(10, 18)
KINDS = 18
FIRST, USUAL, LAST = range(3)
ALL = pl.ds(0, 2 * N)
TOP = pl.ds(0, N)
BOT = pl.ds(N, N)


def dft_tables():
    index = np.arange(N)
    phase = (index[:, None] * index[None, :] % N) * (2.0 * math.pi / N)
    c, s = np.cos(phase) / math.sqrt(N), np.sin(phase) / math.sqrt(N)
    out = []
    for sign in (-1.0, 1.0):
        m = np.block([[c, sign * s], [-sign * s, c]])
        hi = m.astype(ml_dtypes.bfloat16)
        out.append(np.stack([hi, (m - hi.astype(np.float64)).astype(ml_dtypes.bfloat16)]))
    return np.stack(out)


def place(hi_x, lo_x, y, z, core):
    return hi_x * 4 + z, (lo_x * 4 + y) * 2 + core


def parts(gx, gy):
    return lax.div(gx, 4), lax.rem(gx, 4), lax.div(gy, 8), lax.rem(lax.div(gy, 2), 4), lax.rem(gy, 2)


def tile_of(gx, gy):
    hi_x, z, lo_x, y, core = parts(gx, gy)
    lo_x = lax.rem(lo_x + hi_x, 2)
    z = jnp.where(hi_x == 0, 3 - z, z)
    y = jnp.where(lo_x == 1, 3 - y, y)
    return place(hi_x, lo_x, y, z, core)


def device_of(gx, gy):
    hi_x, z, lo_x, y, core = parts(gx, gy)
    z = jnp.where(hi_x == 0, 3 - z, z)
    y = jnp.where(lo_x == 1, 3 - y, y)
    return place(hi_x, lax.rem(lo_x + hi_x, 2), y, z, core)


def cmul(ar, ai, br, bi):
    return ar * br - ai * bi, ar * bi + ai * br


def kernel(
    offs_in, cnt_in, obj, probe_in, prop_in, inten_in, w_in, out,
    o0, o1, d, z, r, a, q, psi, pat, tile, inten, fin, goal, probe, prop, w, offs, cnt,
    ssem, rsem, in_send, in_recv, out_send, out_recv, lsem,
):
    objects = (o0, o1)
    me = (lax.axis_index("gx"), lax.axis_index("gy"))
    gx, gy = tile_of(*me)
    core = lax.rem(gy, 2)
    home = (gx, gy)
    worker = device_of(*me)
    moved = jnp.logical_or(gx != me[0], gy != me[1])
    stays = jnp.logical_not(moved)
    has_u = gx > 0
    has_d = gx < 7
    has_o = jnp.logical_and(gy > 0, gy < 15)
    up = device_of(jnp.maximum(gx - 1, 0), gy)
    dn = device_of(jnp.minimum(gx + 1, 7), gy)
    mate = device_of(gx, gy + 1 - 2 * core)
    outer = device_of(gx, jnp.clip(gy - 1 + 2 * core, 0, 15))
    hl = 1 - core
    hr = core

    lane = lax.broadcasted_iota(jnp.int32, (1, N), 1)
    l_ok = lane >= jnp.where(gy == 0, H, 0)
    r_ok = lane < jnp.where(gy == 15, H, N)

    def desc(kind, src, dst, s, slot, dev):
        return pltpu.make_async_remote_copy(
            src_ref=src,
            dst_ref=dst,
            send_sem=ssem.at[kind, s, slot],
            recv_sem=rsem.at[kind, s, slot],
            device_id=dev,
            device_id_type=MESH,
        )

    def up_rows(mode):
        return {FIRST: (pl.ds(H, H), pl.ds(3 * H, H)), USUAL: (TOP, BOT), LAST: (pl.ds(0, H), pl.ds(N, H))}[mode]

    def down_rows(mode):
        return {FIRST: (pl.ds(N, H), pl.ds(0, H)), USUAL: (BOT, TOP), LAST: (pl.ds(3 * H, H), pl.ds(H, H))}[mode]

    def first_rows(mode):
        return pl.ds(H, N) if mode == FIRST else ALL

    def last_rows(mode):
        return pl.ds(H, N) if mode == LAST else ALL

    def live(kind, s, mode):
        if s == 1:
            return kind < 10
        if kind in (K_YRE_T, K_YRE_B, K_ZIM_U2, K_ZIM_D2, K_ZRE_U2, K_ZRE_D2):
            return mode != FIRST
        if kind in (K_ZRE_U, K_ZRE_D, K_YIM_T, K_YIM_B):
            return mode != LAST
        return True

    def along_z(kind, src, group, s, slot, mode, upward):
        (rows, landing), dev = (up_rows(mode), up) if upward else (down_rows(mode), dn)
        return desc(kind, src.at[rows], r.at[group, s, slot, landing], s, slot, dev)

    def copy(kind, s, slot, mode):
        if kind in (K_YRE, K_YRE_T, K_YRE_B):
            rows = first_rows(FIRST if s == 0 else mode)
            rows = {K_YRE_T: pl.ds(0, H), K_YRE_B: pl.ds(3 * H, H)}.get(kind, rows)
            return desc(kind, d.at[s, 1, 0, rows], r.at[Y_RE, s, slot, rows], s, slot, outer)
        if kind in (K_ZIM_U2, K_ZIM_D2):
            return along_z(kind, d.at[s, 1, 1], Z_IM, s, slot, LAST, kind == K_ZIM_U2)
        if kind in (K_ZRE_U2, K_ZRE_D2):
            return along_z(kind, a.at[0, s], Z_RE, s, slot, LAST, kind == K_ZRE_U2)
        if kind in (K_ZIM_U, K_ZIM_D):
            piece = FIRST if s == 0 or mode == FIRST else USUAL
            return along_z(kind, d.at[s, 1, 1], Z_IM, s, slot, piece, kind == K_ZIM_U)
        if kind == K_M:
            rows = first_rows(mode)
            return desc(kind, d.at[s, 0, 1 - core, rows], r.at[M_RS, s, slot, rows], s, slot, mate)
        if kind in (K_ZM_U, K_ZM_D):
            early = s == 1 and mode == LAST
            return along_z(kind, a.at[2, s], Z_M, s, slot, USUAL if early else mode, kind == K_ZM_U)
        if kind in (K_ZRE_U, K_ZRE_D):
            return along_z(kind, a.at[0, s], Z_RE, s, slot, FIRST if s == 0 else mode, kind == K_ZRE_U)
        rows = last_rows(mode)
        if kind in (K_YIM, K_YIM_T, K_YIM_B):
            rows = pl.ds(H, N) if s == 0 else rows
            rows = {K_YIM_T: pl.ds(0, H), K_YIM_B: pl.ds(3 * H, H)}.get(kind, rows)
            return desc(kind, a.at[1, s, rows], r.at[Y_IM, s, slot, rows], s, slot, outer)
        return desc(kind, objects[s].at[0, core, rows], objects[s].at[0, core, rows], s, slot, mate)

    def landed(kind, s, slot, mode):
        if kind == K_P3:
            rows = last_rows(mode)
            return desc(kind, objects[s].at[0, core, rows], objects[s].at[0, 1 - core, rows], s, slot, mate)
        return copy(kind, s, slot, mode)

    has_no = jnp.logical_not(has_o)
    senders = {
        K_YRE: has_o, K_ZIM_U: has_u, K_ZIM_D: has_d, K_M: None, K_ZM_U: has_u, K_ZM_D: has_d,
        K_ZRE_U: has_u, K_ZRE_D: has_d, K_YIM: has_o, K_P3: None,
        K_YRE_T: has_o, K_YRE_B: has_o, K_ZIM_U2: has_u, K_ZIM_D2: has_d,
        K_ZRE_U2: has_u, K_ZRE_D2: has_d, K_YIM_T: has_o, K_YIM_B: has_o,
    }
    other_way = {K_ZIM_U: K_ZIM_D, K_ZM_U: K_ZM_D, K_ZRE_U: K_ZRE_D, K_ZIM_U2: K_ZIM_D2, K_ZRE_U2: K_ZRE_D2}
    other_way.update({v: k for k, v in other_way.items()})

    def guarded(cond, fn):
        if cond is None:
            fn()
        else:
            pl.when(cond)(fn)

    def send(kind, s, slot, mode):
        if live(kind, s, mode):
            guarded(senders[kind], lambda: copy(kind, s, slot, mode).start())

    def recv(kind, s, slot, mode):
        if live(kind, s, mode):
            guarded(senders[other_way.get(kind, kind)], lambda: landed(kind, s, slot, mode).wait_recv())

    def sent(kind, s, slot, mode):
        if live(kind, s, mode):
            guarded(senders[kind], lambda: copy(kind, s, slot, mode).wait_send())

    def start(s, slot, mode):
        send(K_M, s, slot, mode)
        send(K_YRE, s, slot, mode)
        send(K_ZIM_U, s, slot, mode)
        send(K_ZIM_D, s, slot, mode)

    def mid_m(s, slot, mode):
        recv(K_M, s, slot, mode)
        a[2, s] = d[s, 0, core] + r[M_RS, s, slot]
        send(K_ZM_U, s, slot, mode)
        send(K_ZM_D, s, slot, mode)

    def mid_re(s, slot, mode):
        recv(K_YRE, s, slot, mode)
        a[0, s] = d[s, 1, 0] + r[Y_RE, s, slot]
        send(K_ZRE_U, s, slot, mode)
        send(K_ZRE_D, s, slot, mode)

    def mid_im(s, slot, mode):
        recv(K_ZIM_U, s, slot, mode)
        recv(K_ZIM_D, s, slot, mode)
        a[1, s] = d[s, 1, 1] + r[Z_IM, s, slot]
        send(K_YIM, s, slot, mode)

    def rims_and_middle(mode):
        rims, middle = [pl.ds(0, H), pl.ds(3 * H, H)], [pl.ds(H, N)]
        return (rims, middle) if mode != FIRST else ([], [ALL])

    def re_first(slot, mode):
        recv(K_YRE, 0, slot, mode)
        for rows in rims_and_middle(mode)[1]:
            a[0, 0, rows] = d[0, 1, 0, rows] + r[Y_RE, 0, slot, rows]
        send(K_ZRE_U, 0, slot, mode)
        send(K_ZRE_D, 0, slot, mode)

    def re_second(slot, mode):
        recv(K_YRE_T, 0, slot, mode)
        recv(K_YRE_B, 0, slot, mode)
        for rows in rims_and_middle(mode)[0]:
            a[0, 0, rows] = d[0, 1, 0, rows] + r[Y_RE, 0, slot, rows]
        send(K_ZRE_U2, 0, slot, mode)
        send(K_ZRE_D2, 0, slot, mode)

    def im_first(slot, mode):
        recv(K_ZIM_U2, 0, slot, mode)
        recv(K_ZIM_D2, 0, slot, mode)
        if mode != FIRST:
            a[1, 0, pl.ds(H, N)] = d[0, 1, 1, pl.ds(H, N)] + r[Z_IM, 0, slot, pl.ds(H, N)]
            send(K_YIM, 0, slot, mode)

    def im_second(slot, mode):
        recv(K_ZIM_U, 0, slot, mode)
        recv(K_ZIM_D, 0, slot, mode)
        for rows in [ALL] if mode == FIRST else rims_and_middle(mode)[0]:
            a[1, 0, rows] = d[0, 1, 1, rows] + r[Z_IM, 0, slot, rows]
        send(K_YIM_T, 0, slot, mode)
        send(K_YIM_B, 0, slot, mode)
        if mode == FIRST:
            send(K_YIM, 0, slot, mode)

    def mid_back(s, slot, mode):
        recv(K_ZM_U, s, slot, mode)
        recv(K_ZM_D, s, slot, mode)
        objects[s][0, core] = objects[s][0, core] + (a[2, s] + r[Z_M, s, slot])
        send(K_P3, s, slot, mode)

    def finish(s, slot, mode):
        for kind in (K_ZRE_U, K_ZRE_D, K_ZRE_U2, K_ZRE_D2):
            recv(kind, s, slot, mode)
        objects[s][1, 0] = objects[s][1, 0] + (a[0, s] + r[Z_RE, s, slot])
        for kind in (K_YIM, K_YIM_T, K_YIM_B):
            recv(kind, s, slot, mode)
        objects[s][1, 1] = objects[s][1, 1] + (a[1, s] + r[Y_IM, s, slot])
        recv(K_P3, s, slot, mode)

    def all_sent(slot, mode):
        for s in range(2):
            for kind in range(KINDS):
                sent(kind, s, slot, mode)

    def exchange(slot, mode):
        mid_m(0, slot, mode)
        mid_m(1, slot, USUAL)
        mid_im(1, slot, mode)
        re_first(slot, mode)
        im_first(slot, mode)
        re_second(slot, mode)
        im_second(slot, mode)
        mid_re(1, slot, mode)
        mid_back(0, slot, mode)
        mid_back(1, slot, mode)
        if mode == LAST:
            finish(1, slot, mode)
            give(1)
        all_sent(slot, mode)
        finish(0, slot, mode)

    def send_home(s):
        return pltpu.make_async_remote_copy(
            src_ref=fin.at[s],
            dst_ref=out.at[s],
            send_sem=out_send.at[s],
            recv_sem=out_recv.at[s],
            device_id=home,
            device_id_type=MESH,
        )

    def give(s):
        for c in range(2):
            left = objects[s][hl, c, pl.ds(H, N), :]
            right = objects[s][hr, c, pl.ds(H, N), :]
            fin[s, c] = pltpu.roll(jnp.where(lane >= H, left, right), H, 1)
        pl.when(moved)(lambda: send_home(s).start())

        @pl.when(stays)
        def _():
            out[s] = fin[s]

    inputs = [(offs_in, offs), (cnt_in, cnt)]
    inputs += [(obj.at[s], tile.at[s]) for s in range(2)]

    def pass_on(i, src, dst):
        return pltpu.make_async_remote_copy(
            src_ref=src,
            dst_ref=dst,
            send_sem=in_send.at[i],
            recv_sem=in_recv.at[i],
            device_id=worker,
            device_id_type=MESH,
        )

    def keep(i, src, dst):
        return pltpu.make_async_copy(src, dst, in_send.at[i])

    def pass_start(i, src, dst):
        pl.when(moved)(lambda: pass_on(i, src, dst).start())
        pl.when(stays)(lambda: keep(i, src, dst).start())

    def pass_wait(i, src, dst):
        @pl.when(moved)
        def _():
            pass_on(i, src, dst).wait_send()
            pass_on(i, src, dst).wait_recv()

        pl.when(stays)(lambda: keep(i, src, dst).wait())

    def frames(b):
        return 4 + b, inten_in.at[pl.ds(BATCH * b, BATCH)], inten.at[pl.ds(BATCH * b, BATCH)]

    consts = [(probe_in, probe), (prop_in, prop), (w_in, w)]
    barrier = pltpu.get_barrier_semaphore()
    greet = ((None, mate), (has_u, up), (has_d, dn), (has_o, outer), (moved, home), (moved, worker))
    for cond, dev in greet:
        guarded(cond, lambda dev=dev: pl.semaphore_signal(barrier, inc=1, device_id=dev, device_id_type=MESH))
    for i, (src, dst) in enumerate(consts):
        pltpu.make_async_copy(src, dst, lsem.at[i]).start()
    count = 1 + sum(jnp.where(cond, 1, 0) for cond, _ in greet[1:])
    pl.semaphore_wait(barrier, count)
    for i in (2, 0, 1):
        pass_start(i, *inputs[i])
    for o in objects:
        o[...] = jnp.zeros_like(o)
    d[...] = jnp.zeros_like(d)
    z[...] = jnp.zeros_like(z)
    for group, rows in ((Y_RE, ((0, H), (3 * H, H))), (M_RS, ((0, H), (3 * H, H)))):
        for first, n in rows:
            r[group, :, 0, pl.ds(first, n)] = jnp.zeros((2, n, N), F32)
    for group in (Z_IM, Z_M, Z_RE):
        r[group, :, 0, pl.ds(H, N)] = jnp.zeros((2, N, N), F32)

    @pl.when(gx == 0)
    def _():
        for group in (Z_IM, Z_M, Z_RE):
            r[group, :, :, TOP] = jnp.zeros((2, 2, N, N), F32)

    @pl.when(gx == 7)
    def _():
        for group in (Z_IM, Z_M, Z_RE):
            r[group, :, :, BOT] = jnp.zeros((2, 2, N, N), F32)

    @pl.when(has_no)
    def _():
        for group in (Y_RE, Y_IM):
            r[group] = jnp.zeros((2, 2, 2 * N, N), F32)

    for i, (src, dst) in enumerate(consts):
        pltpu.make_async_copy(src, dst, lsem.at[i]).wait()
    q[0] = jnp.cos(prop[...]).T
    q[1] = jnp.sin(prop[...]).T
    pass_start(3, *inputs[3])

    def begin(s):
        pass_wait(2 + s, *inputs[2 + s])
        for c in range(2):
            cells = pltpu.roll(tile[s, c], H, 1)
            d[s, hl, c, pl.ds(H, N)] = jnp.where(lane >= H, cells, 0.0)
            d[s, hr, c, pl.ds(H, N)] = jnp.where(lane < H, cells, 0.0)
        start(s, 0, FIRST)

    begin(0)
    mid_m(0, 0, FIRST)
    begin(1)
    pass_start(*frames(0))
    re_first(0, FIRST)
    im_second(0, FIRST)
    mid_m(1, 0, FIRST)
    mid_back(0, 0, FIRST)
    mid_re(1, 0, FIRST)
    mid_im(1, 0, FIRST)
    mid_back(1, 0, FIRST)
    for i in range(2):
        pass_wait(i, *inputs[i])
    all_sent(0, FIRST)
    finish(0, 0, FIRST)

    def split(x):
        hi = x.astype(BF16)
        return hi, (x - hi.astype(F32)).astype(BF16)

    def transform(re, im, inverse):
        right = jnp.concatenate([w[inverse, 0], w[inverse, 0], w[inverse, 1]], 0)

        def product(x, y):
            hi, lo = split(jnp.concatenate([x, y], 1))
            z = jnp.dot(jnp.concatenate([hi, lo, hi], 1), right, preferred_element_type=F32)
            return z[:, :N], z[:, N:]

        first = [product(re[m], im[m]) for m in range(BATCH)]
        second = [product(x.T, y.T) for x, y in first]
        return [x for x, _ in second], [y for _, y in second]

    def patch(s, c, r0, q0):
        left = objects[s][hl, c, pl.ds(r0, N), :]
        right = objects[s][hr, c, pl.ds(r0, N), :]
        return pltpu.roll(jnp.where(lane >= q0, left, right), (N - q0) & (N - 1), 1)

    def scatter(s, slot, places, grads):
        for m in range(BATCH):
            r0, q0, weight = places[m]
            fl = jnp.where(jnp.logical_and(lane >= q0, l_ok), weight, 0.0)
            fr = jnp.where(jnp.logical_and(lane < q0, r_ok), weight, 0.0)
            for c in range(2):
                g = pltpu.roll(grads[c][m], q0 & (N - 1), 1)
                z[m, 0, c, pl.ds(N, N)] = g * fl
                z[m, 1, c, pl.ds(N, N)] = g * fr
        for half, side, planes in ((1, core, ((0, (K_YRE, K_YRE_T, K_YRE_B)), (1, (K_ZIM_U2, K_ZIM_D2, K_ZIM_U, K_ZIM_D)))), (0, 1 - core, ((1 - core, (K_M,)), (core, ())))):
            for c, kinds in planes:
                first = z[0, side, c, pl.ds(N - places[0][0], 2 * N), :]
                second = z[1, side, c, pl.ds(N - places[1][0], 2 * N), :]
                d[s, half, c] = first + second

                @pl.when(gx == 0)
                def _():
                    d[s, half, c, pl.ds(0, H)] = jnp.zeros((H, N), F32)

                @pl.when(gx == 7)
                def _():
                    d[s, half, c, pl.ds(3 * H, H)] = jnp.zeros((H, N), F32)

                for kind in kinds:
                    send(kind, s, slot, USUAL)

    def batch(b, carry):
        slot = lax.rem(b + 1, 2)
        before = lax.rem(b, 2)
        pl.when(b < NB - 1)(lambda: pass_start(*frames(b + 1)))
        places = []
        for m in range(BATCH):
            n = b * BATCH + m
            weight = jnp.where(n < cnt[0, 0], -STEP, 0.0).astype(F32)
            places.append((offs[0, n], offs[1, n], weight))
        pr, pi = probe[0], probe[1]
        re, im = [], []
        for m in range(BATCH):
            r0, q0, _ = places[m]
            x, y = cmul(pr, pi, patch(0, 0, r0, q0), patch(0, 1, r0, q0))
            re.append(x)
            im.append(y)
        re, im = transform(re, im, 0)
        both = [cmul(re[m], im[m], q[0], q[1]) for m in range(BATCH)]
        re, im = transform([x for x, _ in both], [y for _, y in both], 1)
        for m in range(BATCH):
            psi[m, 0] = re[m]
            psi[m, 1] = im[m]
        pass_wait(*frames(b))
        for m in range(BATCH):
            goal[m] = inten[b * BATCH + m].T
        pl.when(b == 0)(lambda: finish(1, before, FIRST))
        pl.when(b > 0)(lambda: finish(1, before, USUAL))
        both = []
        for m in range(BATCH):
            r0, q0, _ = places[m]
            for c in range(2):
                pat[m, c] = patch(1, c, r0, q0)
            both.append(cmul(psi[m, 0], psi[m, 1], pat[m, 0], pat[m, 1]))
        re, im = transform([x for x, _ in both], [y for _, y in both], 0)
        excess = [re[m] * re[m] + im[m] * im[m] - goal[m] for m in range(BATCH)]
        re, im = transform([excess[m] * re[m] for m in range(BATCH)], [excess[m] * im[m] for m in range(BATCH)], 1)
        both = [cmul(psi[m, 0], -psi[m, 1], re[m], im[m]) for m in range(BATCH)]
        scatter(1, slot, places, ([x for x, _ in both], [y for _, y in both]))
        both = [cmul(pat[m, 0], -pat[m, 1], re[m], im[m]) for m in range(BATCH)]
        re, im = transform([x for x, _ in both], [y for _, y in both], 0)
        both = [cmul(re[m], im[m], q[0], -q[1]) for m in range(BATCH)]
        re, im = transform([x for x, _ in both], [y for _, y in both], 1)
        both = [cmul(re[m], im[m], pr, -pi) for m in range(BATCH)]
        scatter(0, slot, places, ([x for x, _ in both], [y for _, y in both]))
        pl.when(b < NB - 1)(lambda: exchange(slot, USUAL))
        pl.when(b == NB - 1)(lambda: exchange(slot, LAST))
        return carry

    lax.fori_loop(0, NB, batch, 0)
    give(0)
    for s in range(2):
        @pl.when(moved)
        def _():
            send_home(s).wait_send()
            send_home(s).wait_recv()


def solution(mesh):
    tables = dft_tables()

    def local(object_field, probe, propagator, offsets, counts, intensity):
        hbm = pl.BlockSpec(memory_space=pltpu.HBM)
        return pl.pallas_call(
            kernel,
            out_shape=jax.ShapeDtypeStruct((2, 2, N, N), F32),
            in_specs=[hbm] * 7,
            out_specs=pl.BlockSpec(memory_space=pltpu.VMEM),
            scratch_shapes=[
                pltpu.VMEM((2, 2, 2 * N, N), F32),
                pltpu.VMEM((2, 2, 2 * N, N), F32),
                pltpu.VMEM((2, 2, 2, 2 * N, N), F32),
                pltpu.VMEM((BATCH, 2, 2, 3 * N, N), F32),
                pltpu.VMEM((6, 2, 2, 2 * N, N), F32),
                pltpu.VMEM((3, 2, 2 * N, N), F32),
                pltpu.VMEM((2, N, N), F32),
                pltpu.VMEM((BATCH, 2, N, N), F32),
                pltpu.VMEM((BATCH, 2, N, N), F32),
                pltpu.VMEM((2, 2, N, N), F32),
                pltpu.VMEM((NB * BATCH, N, N), F32),
                pltpu.VMEM((2, 2, N, N), F32),
                pltpu.VMEM((BATCH, N, N), F32),
                pltpu.VMEM((2, N, N), F32),
                pltpu.VMEM((N, N), F32),
                pltpu.VMEM((2, 2, 2 * N, 2 * N), BF16),
                pltpu.SMEM((2, NB * BATCH), jnp.int32),
                pltpu.SMEM((1, 1), jnp.int32),
                pltpu.SemaphoreType.DMA((KINDS, 2, 2)),
                pltpu.SemaphoreType.DMA((KINDS, 2, 2)),
                pltpu.SemaphoreType.DMA((4 + NB,)),
                pltpu.SemaphoreType.DMA((4 + NB,)),
                pltpu.SemaphoreType.DMA((2,)),
                pltpu.SemaphoreType.DMA((2,)),
                pltpu.SemaphoreType.DMA((3,)),
            ],
            compiler_params=pltpu.CompilerParams(
                collective_id=0, has_side_effects=True, vmem_limit_bytes=58 * 1024 * 1024
            ),
        )(
            offsets[0, 0].T, counts, object_field, probe, propagator, intensity[0, 0], jnp.asarray(tables),
        )

    in_specs = (
        P(None, None, "gx", "gy"),
        P(),
        P(),
        P("gx", "gy", None, None),
        P("gx", "gy"),
        P("gx", "gy", None, None, None),
    )
    out_specs = P(None, None, "gx", "gy")
    return jax.shard_map(local, mesh=mesh, in_specs=in_specs, out_specs=out_specs, check_vma=False)
```
